256 devices in a mesh: tm: 8 (over y, core), row: 4 (over x), col: 8 (over z).
Axes of the slice: x: 4, y: 4, z: 8, core: 2. Of those that a mesh axis runs over, the one named last changes fastest.
Arguments:
- frames_in: bfloat16 [32, 96, 256, 128], P('tm', 'row', 'col'), may hold values from -6 to 6
- kernel_base: bfloat16 [3, 3, 3, 128, 128], replicated, may hold values from -0.109375 to 0.109375
- kernel_down: bfloat16 [2, 2, 2, 128, 256], replicated, may hold values from -0.1875 to 0.1875
- kernel_top: bfloat16 [3, 3, 3, 256, 256], replicated, may hold values from -0.078125 to 0.078125
- cotangent: bfloat16 [16, 48, 128, 256], P('tm', 'row', 'col'), may hold values from -6 to 6
Outputs:
- features: bfloat16 [16, 48, 128, 256], P('tm', 'row', 'col')
- grad_frames: float32 [32, 96, 256, 128], P('tm', 'row', 'col')
- grad_base: float32 [27, 128, 128], P(None, 'col', ('tm', 'row'))
- grad_down: float32 [8, 256, 128], P(None, 'col', ('tm', 'row'))
- grad_top: float32 [27, 256, 256], P(None, 'col', ('tm', 'row'))
The draws below stay inside these ranges and needn't reach their ends.
All inputs are finite; a program needn't handle non-finite values.
Results may differ from the reference program's by a relative error of at most 0.025.
Values may be sent and summed in bfloat16 or wider, within the bound.
A program may use at most 192 MiB of HBM per device.

```python
import math
import jax
import jax.numpy as jnp
from jax import lax

C0 = 128
C1 = 256
FRAMES = 32
HEIGHT = 96
WIDTH = 256


def levels(rng, shape, cuts, least, largest):
    level = 1.0
    for axis_at, shards_of in cuts:
        heights = jax.random.uniform(jax.random.fold_in(jax.random.fold_in(rng, 6), axis_at), (shards_of,), jnp.float32, least / len(cuts), largest / len(cuts))
        level = level * jnp.repeat(jnp.exp(heights), shape[axis_at] // shards_of).reshape((-1,) + (1,) * (len(shape) - 1 - axis_at))
    return level


def gaussian(stream_key, extent, scale, most, cuts=(), held_as=jnp.bfloat16):
    values = jax.random.normal(stream_key, extent, jnp.float32) * scale
    if len(cuts) > 0:
        values = levels(stream_key, extent, cuts, -0.22, 0.18) * values
    return jnp.clip(values, min=-most, max=most).astype(held_as)


def setup_inputs(seed: int = 0) -> dict:
    arg_keys = jax.random.split(jax.random.key(seed), 6)
    return {
        "frames_in": gaussian(arg_keys[0], (FRAMES, HEIGHT, WIDTH, C0), 1.0, 6.0, ((0, 8), (1, 4), (2, 8))),
        "kernel_base": gaussian(arg_keys[1], (3, 3, 3, C0, C0), (27 * C0) ** -0.5, 0.109375),
        "kernel_down": gaussian(arg_keys[2], (2, 2, 2, C0, C1), (8 * C0) ** -0.5, 0.1875),
        "kernel_top": gaussian(arg_keys[3], (3, 3, 3, C1, C1), (27 * C1) ** -0.5, 0.078125),
        "cotangent": gaussian(arg_keys[4], (FRAMES // 2, HEIGHT // 2, WIDTH // 2, C1), 1.0, 6.0, ((0, 8), (1, 4), (2, 8))),
    }


numbers = ('NDHWC', 'DHWIO', 'NDHWC')

def conv_valid(padded, kernel):
    return lax.conv_general_dilated(padded[None], kernel, (1, 1, 1), 'VALID', dimension_numbers=numbers, preferred_element_type=jnp.float32)[0]

def down_conv(field, kernel):
    return lax.conv_general_dilated(field[None], kernel, (2, 2, 2), 'VALID', dimension_numbers=numbers, preferred_element_type=jnp.float32)[0]

def flipped(kernel):
    return jnp.transpose(jnp.flip(kernel, (0, 1, 2)), (0, 1, 2, 4, 3))

def causal_pad(field):
    return jnp.pad(field, ((2, 0), (1, 1), (1, 1), (0, 0)))

def anti_pad(field):
    return jnp.pad(field, ((0, 2), (1, 1), (1, 1), (0, 0)))

def silu_slope(pre):
    logistic = jax.nn.sigmoid(pre)
    return logistic * (1.0 + pre * (1.0 - logistic))

def tap_grads(padded, upstream):
    frame_count, row_count, col_count = (upstream.shape[0], upstream.shape[1], upstream.shape[2])
    flat_up = upstream.reshape(-1, upstream.shape[3])
    result = []
    for offset_t in range(3):
        for offset_h in range(3):
            for offset_w in range(3):
                window = padded[offset_t:offset_t + frame_count, offset_h:offset_h + row_count, offset_w:offset_w + col_count]
                window = window.reshape(-1, padded.shape[3])
                result.append(lax.dot_general(flat_up, window, (((0,), (0,)), ((), ())), preferred_element_type=jnp.float32))
    return jnp.stack(result)

def down_back(upstream, kernel):
    frame_count, row_count, col_count, out_channels = upstream.shape
    spread = jnp.einsum('thwo,abcio->tahbwci', upstream.astype(jnp.float32), kernel.astype(jnp.float32))
    return spread.reshape(2 * frame_count, 2 * row_count, 2 * col_count, kernel.shape[3])

def down_grads(field, upstream):
    frame_count, row_count, col_count, out_channels = upstream.shape
    blocks = field.reshape(frame_count, 2, row_count, 2, col_count, 2, field.shape[3])
    result = jnp.einsum('tahbwci,thwo->abcoi', blocks.astype(jnp.float32), upstream.astype(jnp.float32))
    return result.reshape(8, out_channels, field.shape[3])

def reference(frames_in, kernel_base, kernel_down, kernel_top, cotangent):
    base_ext = causal_pad(frames_in)
    pre_base = conv_valid(base_ext, kernel_base)
    hidden = (frames_in.astype(jnp.float32) + jax.nn.silu(pre_base)).astype(jnp.bfloat16)
    reduced = down_conv(hidden, kernel_down).astype(jnp.bfloat16)
    top_ext = causal_pad(reduced)
    pre_top = conv_valid(top_ext, kernel_top)
    features = (reduced.astype(jnp.float32) + jax.nn.silu(pre_top)).astype(jnp.bfloat16)
    upstream = cotangent.astype(jnp.float32)
    slope_top = (upstream * silu_slope(pre_top)).astype(jnp.bfloat16)
    grad_reduced = (upstream + conv_valid(anti_pad(slope_top), flipped(kernel_top))).astype(jnp.bfloat16)
    grad_hidden = down_back(grad_reduced, kernel_down)
    slope_base = (grad_hidden * silu_slope(pre_base)).astype(jnp.bfloat16)
    grad_frames = grad_hidden + conv_valid(anti_pad(slope_base), flipped(kernel_base))
    base_cells = FRAMES * HEIGHT * WIDTH
    top_cells = base_cells // 8
    grad_base = tap_grads(base_ext, slope_base) / math.sqrt(base_cells)
    grad_down = down_grads(hidden, grad_reduced) / math.sqrt(top_cells)
    grad_top = tap_grads(top_ext, slope_top) / math.sqrt(top_cells)
    return (features, grad_frames, grad_base, grad_down, grad_top)
```

```python
import functools
import math
from types import SimpleNamespace

import jax
import jax.numpy as jnp
from jax import lax
from jax.experimental import pallas as pl
from jax.experimental.pallas import tpu as pltpu
from jax.sharding import PartitionSpec as P

F32 = jnp.float32
BF = jnp.bfloat16
ROWS = 20
TOP = 14


def dot(a, b, ca=1, cb=0):
    return lax.dot_general(a, b, (((ca,), (cb,)), ((), ())), preferred_element_type=F32)


def iota(shape, dim):
    return lax.broadcasted_iota(jnp.int32, shape, dim)


def shift_cols(value, by):
    width = value.shape[1]
    rolled = pltpu.roll(value, by % width, 1)
    gap = 0 if by > 0 else width - 1
    return jnp.where(iota(value.shape, 1) == gap, 0.0, rolled)


def pick(parts):
    out = jnp.zeros((parts[0].shape[0], 8, parts[0].shape[2]), F32)
    row = iota(out.shape, 1)
    for t, part in enumerate(parts):
        out = jnp.where(row == t, jnp.broadcast_to(part, out.shape), out)
    return out


def logistic(s):
    return 1.0 / (1.0 + jnp.exp(-s))


def weave(first, second):
    first = first.reshape(16, 8, first.shape[1])
    second = second.reshape(16, 8, second.shape[1])
    low = iota(first.shape, 1) < 4
    even = jnp.where(low, first, pltpu.roll(second, 4, 1))
    odd = jnp.where(low, pltpu.roll(first, 4, 1), second)
    return even, odd


class Halo:
    def __init__(self, comm, body, cols, land, send, recv, frames, height, back, where):
        self.comm, self.body, self.cols, self.land = comm, body, cols, land
        self.send, self.recv, self.back = send, recv, back
        self.frames, self.height, self.where = frames, height, where
        self.own = 0 if back else 2
        self.copies = []

    def start(self):
        tm, row, col = self.where
        step = -1 if self.back else 1
        h, f, own, body = self.height, self.frames, self.own, self.body
        edge = 0 if self.back else own + f - 2
        into = f if self.back else 0
        jobs = []
        for dt in (0, step):
            first, count, put = (own, f, own) if dt == 0 else (edge, 2, into)
            kind = 0 if dt == 0 else 1
            for dh in (0, 1, -1):
                src_h, n, dst_h = {0: (1, h, 1), 1: (h, 1, 0), -1: (1, 1, h + 1)}[dh]
                if dt or dh:
                    jobs.append((kind, (dt, dh, 0),
                                 body.at[pl.ds(first, count), pl.ds(src_h, n)],
                                 body.at[pl.ds(put, count), pl.ds(dst_h, n)]))
                for dw in (1, -1):
                    side = 0 if dw == 1 else 1
                    jobs.append((2, (dt, dh, dw),
                                 self.cols.at[1 - side, pl.ds(src_h - 1, n)],
                                 self.land.at[side, kind, pl.ds(dst_h, n)]))
        if not self.comm:
            return
        for i, (kind, (dt, dh, dw), src, dst) in enumerate(jobs):
            copy = pltpu.make_async_remote_copy(
                src_ref=src, dst_ref=dst, send_sem=self.send.at[i], recv_sem=self.recv.at[i],
                device_id=((tm + dt + 8) % 8, (row + dh + 4) % 4, (col + dw + 8) % 8),
                device_id_type=pl.DeviceIdType.MESH,
            )
            copy.start()
            self.copies.append((kind, copy))

    def wait(self, kind):
        for k, copy in self.copies:
            if k == kind:
                copy.wait_recv()
        row = self.where[1]
        zero = jnp.zeros(self.body.shape[2:], BF)
        frames = range(self.own, self.own + self.frames)
        if kind == 1:
            first = self.frames if self.back else 0
            frames = range(first, first + 2)

            @pl.when(self.where[0] == (7 if self.back else 0))
            def _():
                for t in frames:
                    for r in range(self.height + 2):
                        self.body[t, r] = zero

        if kind < 2:
            @pl.when(row == 0)
            def _():
                for t in frames:
                    self.body[t, 0] = zero

            @pl.when(row == 3)
            def _():
                for t in frames:
                    self.body[t, self.height + 1] = zero

    def column(self, side):
        tm, row, col = self.where
        cur = self.land[side, 0]
        far = self.land[side, 1]
        shape = cur.shape
        at_t, at_h = iota(shape, 1), iota(shape, 0)
        out = col == (7 if side else 0)
        edge = tm == (7 if self.back else 0)
        if self.back:
            is_far = at_t >= self.frames
            far = pltpu.roll(far, self.frames, 1)
        else:
            is_far = at_t < 2
            far = pltpu.roll(far, 8 - (self.frames - 2), 1) if self.frames > 2 else far
            cur = pltpu.roll(cur, 2, 1)
        drop = ((at_h == 0) & (row == 0)) | ((at_h == shape[0] - 1) & (row == 3))
        drop = drop | out | (is_far & edge) | (at_t >= self.frames + 2)
        return jnp.where(drop, 0.0, jnp.where(is_far, far, cur))

    def done(self):
        for _, copy in self.copies:
            copy.wait_send()


class Reduce:
    def __init__(self, comm, s, job, r0, n, where):
        self.comm, self.s, self.job, self.r0, self.n = comm, s, job, r0, n
        tm, row, col = where
        self.y, self.core, self.x, self.z = tm // 2, tm % 2, row, col
        self.half = n // 2
        self.started = []
        self.pending = []
        self.slot = 0

    def put(self, src, dst, y, core, x, z):
        if not self.comm:
            return
        i = self.slot
        self.slot += 1
        copy = pltpu.make_async_remote_copy(
            src_ref=src, dst_ref=dst,
            send_sem=self.s.rs_send.at[self.job, i], recv_sem=self.s.rs_recv.at[self.job, i],
            device_id=(2 * y + core, x, z), device_id_type=pl.DeviceIdType.MESH,
        )
        copy.start()
        self.started.append(copy)
        self.pending.append(copy)

    def arrive(self):
        for copy in self.pending:
            copy.wait_recv()
        self.pending = []

    def a(self):
        return pl.ds(self.r0, self.half)

    def b(self):
        return pl.ds(self.r0 + self.half, self.half)

    def start(self):
        all_r = pl.ds(self.r0, self.n)
        self.put(self.s.terms.at[:, 1 - self.core, :, :, all_r],
                 self.s.c_land.at[:, :, :, all_r], self.y, 1 - self.core, self.x, self.z)

    def planes(self):
        s, y, x = self.s, self.y, self.x
        self.arrive()
        all_r = pl.ds(self.r0, self.n)

        def add(i, _):
            yy, x1, par = i // 4, (i % 4) // 2, i % 2
            s.u[yy, x1, par, all_r] = (
                s.terms[yy, self.core, x1, par, all_r].astype(F32)
                + s.c_land[yy, x1, par, all_r].astype(F32)
            ).astype(BF)
            return _

        lax.fori_loop(0, 16, add, 0)
        for d in (2, 1, 3):
            to = (y + d) % 4
            self.put(s.u.at[to, :, :, self.a()], s.da.at[d - 1, :, :, self.a()],
                     to, self.core, x, self.z)
            to = (x + d) % 4
            self.put(s.u.at[:, to // 2, to % 2, self.b()], s.db.at[d - 1, :, self.b()],
                     y, self.core, to, self.z)

    def lines(self):
        s, y, x = self.s, self.y, self.x
        self.arrive()

        def add(i, _):
            x1, par = i // 2, i % 2
            total = s.u[y, x1, par, self.a()].astype(F32)
            for d in range(3):
                total = total + s.da[d, x1, par, self.a()].astype(F32)
            s.va[x1, par, self.a()] = total.astype(BF)
            total = s.u[i, x // 2, x % 2, self.b()].astype(F32)
            for d in range(3):
                total = total + s.db[d, i, self.b()].astype(F32)
            s.vb[i, self.b()] = total.astype(BF)
            return _

        lax.fori_loop(0, 4, add, 0)
        for d in (2, 1, 3):
            to = (x + d) % 4
            self.put(s.va.at[to // 2, to % 2, self.a()], s.ea.at[d - 1, self.a()],
                     y, self.core, to, self.z)
            to = (y + d) % 4
            self.put(s.vb.at[to, self.b()], s.eb.at[d - 1, self.b()],
                     to, self.core, x, self.z)

    def depth(self):
        s, y, x = self.s, self.y, self.x
        self.arrive()
        first = s.va[x // 2, x % 2, self.a()].astype(F32)
        second = s.vb[y, self.b()].astype(F32)
        for d in range(3):
            first = first + s.ea[d, self.a()].astype(F32)
            second = second + s.eb[d, self.b()].astype(F32)
        rows = self.half * 16
        both = jnp.concatenate([first.reshape(rows, 256), second.reshape(rows, 256)], axis=0)
        if self.job == 0:
            wide = jnp.concatenate([both, jnp.zeros((32, 256), F32)], axis=0).T
            s.zs[0] = wide.astype(BF).reshape(8, 32, 256)
        else:
            down = jnp.concatenate([both[:32], jnp.zeros((96, 256), F32)], axis=0).T
            base = jnp.concatenate([both[32:], jnp.zeros((64, 256), F32)], axis=0).T
            s.zs[1, :, :, :128] = down.astype(BF).reshape(8, 32, 128)
            s.zs[1, :, :16, 128:] = base[:128].astype(BF).reshape(8, 16, 128)
            s.zs[1, :, 16:, 128:] = base[128:].astype(BF).reshape(8, 16, 128)
        for d in (4, 3, 5, 2, 6, 1, 7):
            to = (self.z + d) % 8
            self.put(s.zs.at[self.job, to], s.zr.at[self.job, d - 1], y, self.core, x, to)

    def finish(self, out):
        self.arrive()
        total = self.s.zs[self.job, self.z].astype(F32)
        if self.comm:
            for d in range(7):
                total = total + self.s.zr[self.job, d].astype(F32)
        out[self.job] = total

    def done(self):
        for copy in self.started:
            copy.wait_send()


def scratch_list():
    dma = pltpu.SemaphoreType.DMA
    return dict(
        xe=((6, 26, 32, 128), BF),
        ge=((6, 26, 32, 128), BF),
        wf=((9, 128, 384), BF),
        wb=((384, 1152), BF),
        kd=((1024, 256), BF),
        kt=((27, 256, 256), BF),
        cot=((384, 256), BF),
        pre=((4, 768, 128), F32),
        hg=((4, 12, 2, 32, 128), F32),
        hc=((2, 2, 2, 12, 2, 16, 128), BF),
        s3=((4, 768, 384), BF),
        colx=((2, 192, 1152), BF),
        hl=((2, 192, 128), F32),
        acc=((9, 128, 384), F32),
        xt=((3, 4, 14, 16, 256), BF),
        gt=((3, 4, 14, 16, 256), BF),
        acc_t=((384, 256), F32),
        grd=((384, 256), BF),
        px=((2, 24, 8, 128), F32),
        pg=((2, 24, 8, 128), F32),
        lx=((2, 2, 26, 8, 128), F32),
        lg=((2, 2, 26, 8, 128), F32),
        pxt=((2, 12, 8, 256), F32),
        pgt=((2, 12, 8, 256), F32),
        lxt=((2, 2, 14, 8, 256), F32),
        lgt=((2, 2, 14, 8, 256), F32),
        terms=((4, 2, 2, 2, ROWS, 16, 256), BF),
        c_land=((4, 2, 2, ROWS, 16, 256), BF),
        u=((4, 2, 2, ROWS, 16, 256), BF),
        da=((3, 2, 2, ROWS, 16, 256), BF),
        db=((3, 4, ROWS, 16, 256), BF),
        va=((2, 2, ROWS, 16, 256), BF),
        vb=((4, ROWS, 16, 256), BF),
        ea=((3, ROWS, 16, 256), BF),
        eb=((3, ROWS, 16, 256), BF),
        zs=((2, 8, 32, 256), BF),
        zr=((2, 7, 32, 256), BF),
        local=dma((8,)),
        h_send=dma((4, 17)),
        h_recv=dma((4, 17)),
        rs_send=dma((2, 20)),
        rs_recv=dma((2, 20)),
    )


def base_conv(src, t, weights, turned, chunk):
    width = 384

    def part(h0, n):
        lhs = jnp.concatenate(
            [src[t + a, pl.ds(h0 + b, n)].reshape(n * 32, 128) for a in range(3) for b in range(3)],
            axis=1,
        )
        y = dot(lhs, weights, 1, 1 if turned else 0).reshape(n, 32, width)
        return y[..., 128:256] + shift_cols(y[..., :128], 1) + shift_cols(y[..., 256:], -1)

    return part


def kernel(comm, skip, frames, kb, kd, kt, cot, feat, gf, zout, *refs):
    names = list(scratch_list())
    s = SimpleNamespace(**dict(zip(names, refs)))
    if comm:
        where = (lax.axis_index("tm"), lax.axis_index("row"), lax.axis_index("col"))
    else:
        where = (jnp.int32(0), jnp.int32(0), jnp.int32(0))
    tm, row, col = where
    loads = [
        pltpu.make_async_copy(frames, s.xe.at[pl.ds(2, 4), pl.ds(1, 24)], s.local.at[0]),
        pltpu.make_async_copy(kb.at[:, 0], s.wf.at[:, :, pl.ds(0, 128)], s.local.at[1]),
        pltpu.make_async_copy(kb.at[:, 1], s.wf.at[:, :, pl.ds(128, 128)], s.local.at[2]),
        pltpu.make_async_copy(kb.at[:, 2], s.wf.at[:, :, pl.ds(256, 128)], s.local.at[3]),
        pltpu.make_async_copy(kd, s.kd, s.local.at[4]),
        pltpu.make_async_copy(kt, s.kt, s.local.at[5]),
        pltpu.make_async_copy(cot, s.cot, s.local.at[6]),
    ]
    for load in loads:
        load.start()
    halo_x = Halo(comm, s.xe, s.px, s.lx, s.h_send.at[0], s.h_recv.at[0], 4, 24, False, where)
    halo_xt = Halo(comm, s.xt.at[1], s.pxt, s.lxt, s.h_send.at[1], s.h_recv.at[1], 2, 12, False, where)
    halo_gt = Halo(comm, s.gt.at[1], s.pgt, s.lgt, s.h_send.at[2], s.h_recv.at[2], 2, 12, True, where)
    halo_g = Halo(comm, s.ge, s.pg, s.lg, s.h_send.at[3], s.h_recv.at[3], 4, 24, True, where)
    rs_top = Reduce(comm, s, 0, 0, TOP, where)
    rs_low = Reduce(comm, s, 1, TOP, ROWS - TOP, where)

    if comm:
        barrier = pltpu.get_barrier_semaphore()
        near = [(a, b, c) for a in (0, 1, -1) for b in (0, 1, -1) for c in (0, 1, -1)][1:]
        far = [(2, 0, 0), (4, 0, 0), (6, 0, 0), (0, 2, 0)] + [(0, 0, d) for d in (2, 3, 4, 5, 6)]
        for dt, dh, dw in near + far:
            pl.semaphore_signal(
                barrier, inc=1,
                device_id=((tm + dt + 8) % 8, (row + dh + 4) % 4, (col + dw + 8) % 8),
                device_id_type=pl.DeviceIdType.MESH,
            )
    loads[0].wait()
    left, right = [], []
    for t in range(4):
        left.append(s.xe[2 + t, pl.ds(1, 24), pl.ds(0, 16)].astype(F32)[:, 0:1])
        right.append(s.xe[2 + t, pl.ds(1, 24), pl.ds(16, 16)].astype(F32)[:, 15:16])
    s.px[0] = pick(left)
    s.px[1] = pick(right)
    if comm:
        pl.semaphore_wait(barrier, len(near) + len(far))
    halo_x.start()

    for load in loads[1:4]:
        load.wait()
    for ab in range(9):
        for c in range(3):
            s.wb[c * 128:(c + 1) * 128, ab * 128:(ab + 1) * 128] = (
                s.wf[8 - ab, :, (2 - c) * 128:(3 - c) * 128])
    for load in loads[4:]:
        load.wait()

    weights = s.wf[...].reshape(1152, 384)

    def forward(i, _):
        t, h0 = i // 3, (i % 3) * 8
        value = base_conv(s.xe, t, s.wf[...].reshape(1152, 384), False, 8)(h0, 8)
        s.pre[t, pl.ds(pl.multiple_of(h0 * 32, 256), 256)] = value.reshape(256, 128)
        return _

    if "fwd" not in skip:
        halo_x.wait(0)
        lax.fori_loop(6, 12, forward, 0)
        halo_x.wait(1)
        lax.fori_loop(0, 6, forward, 0)
        halo_x.wait(2)
    for side in range(2):
        column = halo_x.column(side)
        pieces = []
        for a in range(3):
            moved = pltpu.roll(column, 8 - a, 1) if a else column
            for b in range(3):
                pieces.append(moved[b:b + 24].reshape(192, 128).astype(BF))
        lhs = jnp.concatenate(pieces, axis=1)
        s.colx[side] = lhs
        c = 2 * side
        s.hl[side] = dot(lhs, s.wf[:, :, c * 128:(c + 1) * 128].reshape(1152, 128))
    for t in range(4):
        for side in range(2):
            at = pl.ds(31 * side, 24, stride=32)
            s.pre[t, at] = s.pre[t, at] + s.hl[side, pl.ds(t, 24, stride=8)]

    def act(i, _):
        t, h1 = i // 12, i % 12
        rows = pl.ds(pl.multiple_of(h1 * 64, 64), 64)
        pre = s.pre[t, rows]
        q = logistic(pre)
        x = s.xe[2 + t, pl.ds(1 + 2 * h1, 2)].reshape(64, 128).astype(F32)
        hidden = (x + pre * q).astype(BF).astype(F32)
        s.hg[t, h1] = hidden.reshape(2, 32, 128)
        s.pre[t, rows] = q * (1.0 + pre * (1.0 - q))
        return _

    lax.fori_loop(0, 48, act, 0)
    for t in range(4):
        for c in range(2):
            s.hc[c, t // 2, t % 2] = s.hg[t, :, :, pl.ds(c, 16, stride=2), :].astype(BF)
    taps = [(a, b, c) for a in range(2) for b in range(2) for c in range(2)]
    lhs = jnp.concatenate([s.hc[c, :, a, :, b].reshape(384, 128) for a, b, c in taps], axis=1)
    reduced = dot(lhs, s.kd[...]).astype(BF)
    red32 = reduced.astype(F32).reshape(2, 12, 16, 256)
    s.xt[1, pl.ds(2, 2), pl.ds(1, 12)] = reduced.reshape(2, 12, 16, 256)
    for side, w in ((0, 0), (1, 15)):
        s.pxt[side] = pick([red32[t, :, w:w + 1] for t in range(2)])
    halo_xt.start()

    def sides(halo, ext):
        for side in range(2):
            column = halo.column(side)
            for t in range(4):
                body = ext[1, t].astype(F32)
                rolled = pltpu.roll(body, 15 if side else 1, 1)
                edge = jnp.broadcast_to(column[:, t:t + 1], body.shape)
                put = jnp.where(iota(body.shape, 1) == (15 if side else 0), edge, rolled)
                ext[2 * side, t] = put.astype(BF)

    for kind in range(3):
        halo_xt.wait(kind)
    sides(halo_xt, s.xt)

    def top_conv(ext, turned):
        s.acc_t[...] = jnp.zeros((384, 256), F32)

        def step(ab, _):
            a, b = ab // 3, ab % 3
            total = s.acc_t[...]
            for c in range(3):
                lhs = ext[c, pl.ds(a, 2), pl.ds(b, 12)].reshape(384, 256)
                if turned:
                    total = total + dot(lhs, s.kt[26 - (ab * 3 + c)], 1, 1)
                else:
                    total = total + dot(lhs, s.kt[ab * 3 + c])
            s.acc_t[...] = total
            return _

        lax.fori_loop(0, 9, step, 0)
        return s.acc_t[...]

    if "top" not in skip:
        top_conv(s.xt, False)
    pre_top = s.acc_t[...]
    q = logistic(pre_top)
    red = s.xt[1, pl.ds(2, 2), pl.ds(1, 12)].reshape(384, 256).astype(F32)
    feat[...] = (red + pre_top * q).astype(BF)
    up = s.cot[...].astype(F32)
    slope = (up * (q * (1.0 + pre_top * (1.0 - q)))).astype(BF)
    s.grd[...] = slope
    slope32 = slope.astype(F32).reshape(2, 12, 16, 256)
    s.gt[1, pl.ds(0, 2), pl.ds(1, 12)] = slope.reshape(2, 12, 16, 256)
    for side, w in ((0, 0), (1, 15)):
        s.pgt[side] = pick([slope32[t, :, w:w + 1] for t in range(2)])
    halo_gt.start()

    def top_tap(tap):
        a, b, c = tap // 9, (tap // 3) % 3, tap % 3
        window = s.xt[c, pl.ds(a, 2), pl.ds(b, 12)].reshape(384, 256)
        return dot(window, s.grd[...], 0, 0).reshape(32, 8, 256)

    def top_pair(r, _):
        both = jnp.concatenate([top_tap(2 * r), top_tap(2 * r + 1)], axis=1)
        s.terms[:, :, :, :, r] = both.astype(BF).reshape(4, 2, 2, 2, 16, 256)
        return _

    if "tgrad" not in skip:
        lax.fori_loop(0, 13, top_pair, 0)
    both = jnp.concatenate([top_tap(26), jnp.zeros((32, 8, 256), F32)], axis=1)
    s.terms[:, :, :, :, 13] = both.astype(BF).reshape(4, 2, 2, 2, 16, 256)
    rs_top.start()

    for kind in range(3):
        halo_gt.wait(kind)
    sides(halo_gt, s.gt)
    if "top" not in skip:
        top_conv(s.gt, True)
    grad_red = (s.cot[...].astype(F32) + s.acc_t[...]).astype(BF)
    s.grd[...] = grad_red
    spread = dot(grad_red, s.kd[...], 1, 1)
    for i, (a, b, c) in enumerate(taps):
        part = spread[:, i * 128:(i + 1) * 128].reshape(2, 12, 16, 128)
        for t in range(2):
            s.hg[2 * t + a, :, b, pl.ds(c, 16, stride=2), :] = part[t]

    low, high = [], []
    for t in range(4):
        gh = s.hg[t].reshape(24, 32, 128)
        slope = (gh * s.pre[t].reshape(24, 32, 128)).astype(BF)
        s.ge[t, pl.ds(1, 24)] = slope
        slope32 = slope.astype(F32)
        low.append(slope32[:, 0:1])
        high.append(slope32[:, 31:32])
        s.s3[t, :, 128:256] = slope.reshape(768, 128)
        s.s3[t, :, :128] = shift_cols(slope32, -1).astype(BF).reshape(768, 128)
        s.s3[t, :, 256:] = shift_cols(slope32, 1).astype(BF).reshape(768, 128)
    s.pg[0] = pick(low)
    s.pg[1] = pick(high)
    halo_g.start()
    rs_top.planes()

    def store_low(r, lanes, group):
        first, second = weave(group[0], group[1]), weave(group[2], group[3])
        for par in range(2):
            both = jnp.concatenate([first[par], second[par]], axis=1).astype(BF)
            s.terms[:, :, :, par, r, :, lanes] = both.reshape(4, 2, 2, 16, both.shape[2])

    for g in range(2):
        group = [
            dot(s.hc[c, :, a, :, b].reshape(384, 128), s.grd[...], 0, 0)
            for a, b, c in taps[4 * g:4 * g + 4]
        ]
        store_low(TOP + g, slice(0, 256), group)

    def base_tap(ab, _):
        a, b = ab // 3, ab % 3
        total = jnp.zeros((128, 384), F32)
        for t in range(4):
            window = s.xe[t + a, pl.ds(b, 24)].reshape(768, 128)
            total = total + dot(window, s.s3[t], 0, 0)
        s.acc[ab] = total
        return _

    if "bgrad" not in skip:
        lax.fori_loop(0, 9, base_tap, 0)
    for side in range(2):
        extra = dot(s.colx[side], s.pg[side].reshape(192, 128).astype(BF), 0, 0)
        lanes = slice(256 * side, 256 * side + 128)
        s.acc[:, :, lanes] = s.acc[:, :, lanes] + extra.reshape(9, 128, 128)
    for g in range(7):
        group = []
        for tap in range(4 * g, 4 * g + 4):
            if tap < 27:
                c = tap % 3
                group.append(s.acc[tap // 3, :, c * 128:(c + 1) * 128])
            else:
                group.append(jnp.zeros((128, 128), F32))
        store_low(TOP + 2 + g // 2, slice(128 * (g % 2), 128 * (g % 2) + 128), group)
    s.terms[:, :, :, :, ROWS - 1, :, 128:] = jnp.zeros((4, 2, 2, 2, 16, 128), BF)
    rs_low.start()
    rs_top.lines()

    for kind in range(3):
        halo_g.wait(kind)
    rs_low.planes()

    def backward(i, _):
        t, h0 = i // 3, (i % 3) * 8
        value = base_conv(s.ge, t, s.wb[...], True, 8)(h0, 8)
        gh = s.hg[t].reshape(24, 32, 128) if False else s.hg[t, pl.ds(h0 // 2, 4)].reshape(256, 128)
        gf[t, pl.ds(pl.multiple_of(h0 * 32, 256), 256)] = gh + value.reshape(256, 128)
        return _

    if "bwd" not in skip:
        lax.fori_loop(0, 6, backward, 0)
    rs_top.depth()
    rs_low.lines()
    if "bwd" not in skip:
        lax.fori_loop(6, 12, backward, 0)
    for side in range(2):
        column = halo_g.column(side)
        pieces = []
        for a in range(3):
            moved = pltpu.roll(column, 8 - a, 1) if a else column
            for b in range(3):
                pieces.append(moved[b:b + 24].reshape(192, 128).astype(BF))
        lhs = jnp.concatenate(pieces, axis=1)
        c = 2 * side
        s.hl[side] = dot(lhs, s.wb[c * 128:(c + 1) * 128, :], 1, 1)
    for t in range(4):
        for side in range(2):
            at = pl.ds(31 * side, 24, stride=32)
            gf[t, at] = gf[t, at] + s.hl[side, pl.ds(t, 24, stride=8)]
    rs_low.depth()
    rs_top.finish(zout)
    rs_low.finish(zout)
    for user in (halo_x, halo_xt, halo_gt, halo_g, rs_top, rs_low):
        user.done()


def call(comm, skip, *args):
    scratch = [pltpu.VMEM(*v) if isinstance(v, tuple) else v for v in scratch_list().values()]
    vmem = pl.BlockSpec(memory_space=pltpu.VMEM)
    params = dict(collective_id=0, has_side_effects=True) if comm else {}
    return pl.pallas_call(
        functools.partial(kernel, comm, skip),
        out_shape=(
            jax.ShapeDtypeStruct((384, 256), BF),
            jax.ShapeDtypeStruct((4, 768, 128), F32),
            jax.ShapeDtypeStruct((2, 32, 256), F32),
        ),
        in_specs=[pl.BlockSpec(memory_space=pl.ANY)] * 5,
        out_specs=(vmem, vmem, vmem),
        scratch_shapes=scratch,
        compiler_params=pltpu.CompilerParams(vmem_limit_bytes=60 * 1024 * 1024, **params),
        cost_estimate=pl.CostEstimate(flops=13 * 10**9, bytes_accessed=10**7, transcendentals=10**6),
    )(*args)


def unpack(zout, base_cells, top_cells):
    top = zout[0].reshape(32, 32, 8)[:, :27].transpose(1, 0, 2) / math.sqrt(top_cells)
    down = zout[1, :, :32].reshape(32, 8, 4).transpose(1, 0, 2) / math.sqrt(top_cells)
    base = zout[1, :, 128:192].reshape(2, 16, 4, 4, 4).transpose(2, 0, 3, 1, 4)
    base = base.reshape(32, 16, 4)[:27] / math.sqrt(base_cells)
    return base, down, top


def body(frames_in, kernel_base, kernel_down, kernel_top, cotangent, comm=True, skip=()):
    feat, gf, zout = call(
        comm, skip,
        frames_in,
        kernel_base.reshape(9, 3, 128, 128),
        kernel_down.reshape(1024, 256),
        kernel_top.reshape(27, 256, 256),
        cotangent.reshape(384, 256),
    )
    devices = 1
    if comm:
        devices = lax.axis_size("tm") * lax.axis_size("row") * lax.axis_size("col")
    base, down, top = unpack(zout, devices * 3072, devices * 384)
    return feat.reshape(2, 12, 16, 256), gf.reshape(4, 24, 32, 128), base, down, top


def solution(mesh):
    return jax.shard_map(
        body,
        mesh=mesh,
        in_specs=(P("tm", "row", "col", None), P(), P(), P(), P("tm", "row", "col", None)),
        out_specs=(
            P("tm", "row", "col", None),
            P("tm", "row", "col", None),
            P(None, "col", ("tm", "row")),
            P(None, "col", ("tm", "row")),
            P(None, "col", ("tm", "row")),
        ),
        check_vma=False,
    )
```

```python
import functools
import math
from types import SimpleNamespace

import jax
import jax.numpy as jnp
from jax import lax
from jax.experimental import pallas as pl
from jax.experimental.pallas import tpu as pltpu
from jax.sharding import PartitionSpec as P

F32 = jnp.float32
BF = jnp.bfloat16
ROWS = 20
TOP = 14


def dot(a, b, ca=1, cb=0):
    return lax.dot_general(a, b, (((ca,), (cb,)), ((), ())), preferred_element_type=F32)


def iota(shape, dim):
    return lax.broadcasted_iota(jnp.int32, shape, dim)


def shift_cols(value, by):
    width = value.shape[1]
    rolled = pltpu.roll(value, by % width, 1)
    gap = 0 if by > 0 else width - 1
    return jnp.where(iota(value.shape, 1) == gap, 0.0, rolled)


def pick(parts):
    out = jnp.zeros((parts[0].shape[0], 8, parts[0].shape[2]), F32)
    row = iota(out.shape, 1)
    for t, part in enumerate(parts):
        out = jnp.where(row == t, jnp.broadcast_to(part, out.shape), out)
    return out


def pack(value):
    h, _, c = value.shape
    pairs = value.reshape(h // 2, 2, 8, c)
    both = pairs[:, 0] + pltpu.roll(pairs[:, 1], 4, 1)
    return both.reshape(h // 4, 16, c).astype(BF)


def unpack_rows(groups, h):
    g, _, c = groups.shape
    pairs = groups.astype(F32).reshape(2 * g, 8, c)
    low = iota(pairs.shape, 1) < 4
    even = jnp.where(low, pairs, 0.0)
    odd = jnp.where(low, pltpu.roll(pairs, 4, 1), 0.0)
    rows = jnp.stack([even, odd], axis=1).reshape(4 * g, 8, c)
    return rows[3:h + 5]


def logistic(s):
    return 1.0 / (1.0 + jnp.exp(-s))


def weave(first, second):
    first = first.reshape(16, 8, first.shape[1])
    second = second.reshape(16, 8, second.shape[1])
    low = iota(first.shape, 1) < 4
    even = jnp.where(low, first, pltpu.roll(second, 4, 1))
    odd = jnp.where(low, pltpu.roll(first, 4, 1), second)
    return even, odd


class Halo:
    def __init__(self, comm, body, cols, land, send, recv, frames, height, back, where):
        self.comm, self.body, self.cols, self.land = comm, body, cols, land
        self.send, self.recv, self.back = send, recv, back
        self.frames, self.height, self.where = frames, height, where
        self.own = 0 if back else 2
        self.copies = []

    def start(self):
        tm, row, col = self.where
        step = -1 if self.back else 1
        h, f, own, body = self.height, self.frames, self.own, self.body
        edge = 0 if self.back else own + f - 2
        into = f if self.back else 0
        jobs = []
        for dt in (0, step):
            first, count, put = (own, f, own) if dt == 0 else (edge, 2, into)
            kind = 0 if dt == 0 else 1
            for dh in (0, 1, -1):
                src_h, n, dst_h = {0: (1, h, 1), 1: (h, 1, 0), -1: (1, 1, h + 1)}[dh]
                if dt or dh:
                    jobs.append((kind, (dt, dh, 0),
                                 body.at[pl.ds(first, count), pl.ds(src_h, n)],
                                 body.at[pl.ds(put, count), pl.ds(dst_h, n)]))
                g = h // 4
                src_g, n_g, dst_g = {0: (0, g, 1), 1: (g - 1, 1, 0), -1: (0, 1, g + 1)}[dh]
                for dw in (1, -1):
                    side = 0 if dw == 1 else 1
                    jobs.append((2, (dt, dh, dw),
                                 self.cols.at[1 - side, pl.ds(src_g, n_g)],
                                 self.land.at[side, kind, pl.ds(dst_g, n_g)]))
        jobs.sort(key=lambda job: job[0])
        if not self.comm:
            return
        for i, (kind, (dt, dh, dw), src, dst) in enumerate(jobs):
            copy = pltpu.make_async_remote_copy(
                src_ref=src, dst_ref=dst, send_sem=self.send.at[i], recv_sem=self.recv.at[i],
                device_id=((tm + dt + 8) % 8, (row + dh + 4) % 4, (col + dw + 8) % 8),
                device_id_type=pl.DeviceIdType.MESH,
            )
            copy.start()
            self.copies.append((kind, copy))

    def wait(self, kind):
        for k, copy in self.copies:
            if k == kind:
                copy.wait_recv()
        row = self.where[1]
        zero = jnp.zeros(self.body.shape[2:], BF)
        frames = range(self.own, self.own + self.frames)
        if kind == 1:
            first = self.frames if self.back else 0
            frames = range(first, first + 2)

            @pl.when(self.where[0] == (7 if self.back else 0))
            def _():
                for t in frames:
                    for r in range(self.height + 2):
                        self.body[t, r] = zero

        if kind < 2:
            @pl.when(row == 0)
            def _():
                for t in frames:
                    self.body[t, 0] = zero

            @pl.when(row == 3)
            def _():
                for t in frames:
                    self.body[t, self.height + 1] = zero

    def column(self, side):
        tm, row, col = self.where
        cur = unpack_rows(self.land[side, 0], self.height)
        far = unpack_rows(self.land[side, 1], self.height)
        shape = cur.shape
        at_t, at_h = iota(shape, 1), iota(shape, 0)
        out = col == (7 if side else 0)
        edge = tm == (7 if self.back else 0)
        if self.back:
            is_far = at_t >= self.frames
            far = pltpu.roll(far, self.frames, 1)
        else:
            is_far = at_t < 2
            far = pltpu.roll(far, 8 - (self.frames - 2), 1) if self.frames > 2 else far
            cur = pltpu.roll(cur, 2, 1)
        drop = ((at_h == 0) & (row == 0)) | ((at_h == shape[0] - 1) & (row == 3))
        drop = drop | out | (is_far & edge) | (at_t >= self.frames + 2)
        return jnp.where(drop, 0.0, jnp.where(is_far, far, cur))

    def done(self):
        for _, copy in self.copies:
            copy.wait_send()


class Reduce:
    def __init__(self, comm, s, job, r0, n, where):
        self.comm, self.s, self.job, self.r0, self.n = comm, s, job, r0, n
        tm, row, col = where
        self.y, self.core, self.x, self.z = tm // 2, tm % 2, row, col
        self.half = n // 2
        self.started = []
        self.pending = []
        self.slot = 0

    def put(self, src, dst, y, core, x, z):
        if not self.comm:
            return
        i = self.slot
        self.slot += 1
        copy = pltpu.make_async_remote_copy(
            src_ref=src, dst_ref=dst,
            send_sem=self.s.rs_send.at[self.job, i], recv_sem=self.s.rs_recv.at[self.job, i],
            device_id=(2 * y + core, x, z), device_id_type=pl.DeviceIdType.MESH,
        )
        copy.start()
        self.started.append(copy)
        self.pending.append(copy)

    def arrive(self):
        for copy in self.pending:
            copy.wait_recv()
        self.pending = []

    def a(self):
        return pl.ds(self.r0, self.half)

    def b(self):
        return pl.ds(self.r0 + self.half, self.half)

    def start(self, r0, n):
        all_r = pl.ds(r0, n)
        self.put(self.s.terms.at[:, 1 - self.core, :, :, all_r],
                 self.s.c_land.at[:, :, :, all_r], self.y, 1 - self.core, self.x, self.z)

    def planes(self):
        s, y, x = self.s, self.y, self.x
        self.arrive()
        all_r = pl.ds(self.r0, self.n)

        def add(i, _):
            yy, x1, par = i // 4, (i % 4) // 2, i % 2
            s.u[yy, x1, par, all_r] = (
                s.terms[yy, self.core, x1, par, all_r].astype(F32)
                + s.c_land[yy, x1, par, all_r].astype(F32)
            ).astype(BF)
            return _

        lax.fori_loop(0, 16, add, 0)
        if self.job == 0:
            up, down, opp = (y + 1) % 4, (y + 3) % 4, (y + 2) % 4
            east, west, over = (x + 1) % 4, (x + 3) % 4, (x + 2) % 4
            p, q, p2, q2 = self.quarters()

            def along_y(to, unit, r, land):
                self.put(s.u.at[unit, :, :, r], s.da.at[land, :, :, r], to, self.core, x, self.z)

            def along_x(to, unit, r, land):
                self.put(s.u.at[:, unit // 2, unit % 2, r], s.db.at[land, :, r],
                         y, self.core, to, self.z)

            along_y(up, opp, p, 0)
            along_y(down, opp, q, 0)
            along_x(east, over, p2, 0)
            along_x(west, over, q2, 0)
            self.later, self.pending = [], self.pending
            first = self.pending
            self.pending = []
            along_y(up, up, q, 1)
            along_y(down, down, p, 1)
            along_x(east, east, q2, 1)
            along_x(west, west, p2, 1)
            self.later, self.pending = self.pending, first
            return
        for d in (2, 1, 3):
            to = (y + d) % 4
            self.put(s.u.at[to, :, :, self.a()], s.da.at[d - 1, :, :, self.a()],
                     to, self.core, x, self.z)
            to = (x + d) % 4
            self.put(s.u.at[:, to // 2, to % 2, self.b()], s.db.at[d - 1, :, self.b()],
                     y, self.core, to, self.z)

    def quarters(self):
        r, n = self.r0, self.n // 4
        return tuple(pl.ds(r + i * n, n) for i in range(4))

    def relay(self):
        s, y, x = self.s, self.y, self.x
        self.arrive()
        up, down, east, west = (y + 1) % 4, (y + 3) % 4, (x + 1) % 4, (x + 3) % 4
        p, q, p2, q2 = self.quarters()

        def add(i, _):
            x1, par = i // 2, i % 2
            for to, r in ((up, p), (down, q)):
                s.g[0, x1, par, r] = (
                    s.u[to, x1, par, r].astype(F32) + s.da[0, x1, par, r].astype(F32)).astype(BF)
            for to, r in ((east, p2), (west, q2)):
                s.g[1, x1, par, r] = (
                    s.u[i, to // 2, to % 2, r].astype(F32) + s.db[0, i, r].astype(F32)).astype(BF)
            return _

        lax.fori_loop(0, 4, add, 0)
        self.put(s.g.at[0, :, :, p], s.da.at[2, :, :, p], up, self.core, x, self.z)
        self.put(s.g.at[0, :, :, q], s.da.at[2, :, :, q], down, self.core, x, self.z)
        self.put(s.g.at[1, :, :, p2], s.dc.at[:, :, p2], y, self.core, east, self.z)
        self.put(s.g.at[1, :, :, q2], s.dc.at[:, :, q2], y, self.core, west, self.z)
        self.pending = self.pending + self.later

    def lines(self):
        s, y, x = self.s, self.y, self.x
        self.arrive()

        def add(i, _):
            x1, par = i // 2, i % 2
            total = s.u[y, x1, par, self.a()].astype(F32)
            for d in range(1 if self.job == 0 else 0, 3):
                total = total + s.da[d, x1, par, self.a()].astype(F32)
            s.va[x1, par, self.a()] = total.astype(BF)
            total = s.u[i, x // 2, x % 2, self.b()].astype(F32)
            if self.job == 0:
                total = total + s.db[1, i, self.b()].astype(F32)
                total = total + s.dc[x1, par, self.b()].astype(F32)
            else:
                for d in range(3):
                    total = total + s.db[d, i, self.b()].astype(F32)
            s.vb[i, self.b()] = total.astype(BF)
            return _

        lax.fori_loop(0, 4, add, 0)
        for d in (2, 1, 3):
            to = (x + d) % 4
            self.put(s.va.at[to // 2, to % 2, self.a()], s.ea.at[d - 1, self.a()],
                     y, self.core, to, self.z)
            to = (y + d) % 4
            self.put(s.vb.at[to, self.b()], s.eb.at[d - 1, self.b()],
                     to, self.core, x, self.z)

    def depth(self):
        s, y, x = self.s, self.y, self.x
        self.arrive()
        first = s.va[x // 2, x % 2, self.a()].astype(F32)
        second = s.vb[y, self.b()].astype(F32)
        for d in range(3):
            first = first + s.ea[d, self.a()].astype(F32)
            second = second + s.eb[d, self.b()].astype(F32)
        rows = self.half * 16
        both = jnp.concatenate([first.reshape(rows, 256), second.reshape(rows, 256)], axis=0)
        if self.job == 0:
            s.zs[...] = both.T.astype(BF).reshape(8, 32, 256)
            src, dst = s.zs, s.zr
        else:
            base = jnp.concatenate([both, jnp.zeros((64, 256), F32)], axis=0).T
            s.zs1[:, :16] = base[:128].astype(BF).reshape(8, 16, 128)
            s.zs1[:, 16:] = base[128:].astype(BF).reshape(8, 16, 128)
            src, dst = s.zs1, s.zr1
        for d in (4, 3, 5, 2, 6, 1, 7):
            to = (self.z + d) % 8
            self.put(src.at[to], dst.at[d - 1], y, self.core, x, to)

    def total(self):
        s = self.s
        self.arrive()
        src, dst = (s.zs, s.zr) if self.job == 0 else (s.zs1, s.zr1)
        total = src[self.z].astype(F32)
        if self.comm:
            for d in range(7):
                total = total + dst[d].astype(F32)
        pad = jnp.zeros((96, total.shape[1]), F32)
        return jnp.concatenate([total, pad], axis=0)

    def finish_top(self, top, down, scale):
        turned = self.total().T * scale
        top[...] = turned[:216, :32].reshape(27, 8, 32)
        for tap in range(8):
            down[tap] = turned[224 + 4 * tap:228 + 4 * tap, :32]

    def finish_base(self, out, scale):
        s = self.s
        s.fin[...] = self.total().T * scale
        parts = []
        low = iota((8, 128), 0) < 4
        for k in range(4):
            rows = s.fin[pl.ds(k, 16, stride=4), :]
            beside = pltpu.roll(rows, 112, 1)
            for j in range(2):
                first, second = rows[8 * j:8 * j + 8], beside[8 * j:8 * j + 8]
                parts.append(jnp.where(low, first, pltpu.roll(second, 4, 0)))
                parts.append(jnp.where(low, pltpu.roll(first, 4, 0), second))
        taps = jnp.concatenate(parts, axis=0).T[:16]
        for k in range(4):
            out[:, k, :] = (pltpu.roll(taps, 128 - 32 * k, 1) if k else taps)[:, :27]

    def done(self):
        for copy in self.started:
            copy.wait_send()


def scratch_list():
    dma = pltpu.SemaphoreType.DMA
    return dict(
        xe=((6, 26, 32, 128), BF),
        ge=((6, 26, 32, 128), BF),
        wf=((9, 128, 384), BF),
        wb=((384, 1152), BF),
        kd=((1024, 256), BF),
        kt=((27, 256, 256), BF),
        cot=((384, 256), BF),
        pre=((4, 768, 128), F32),
        hg=((4, 12, 2, 32, 128), F32),
        hc=((2, 2, 2, 12, 2, 16, 128), BF),
        s3=((4, 768, 384), BF),
        colx=((2, 192, 1152), BF),
        hl=((2, 192, 128), F32),
        acc=((9, 128, 384), F32),
        xf=((3, 128, 4608), BF),
        hf=((8, 128, 384), BF),
        xt=((3, 4, 14, 16, 256), BF),
        gt=((3, 4, 14, 16, 256), BF),
        acc_t=((384, 256), F32),
        grd=((384, 256), BF),
        sg=((2, 192, 128), BF),
        px=((2, 6, 16, 128), BF),
        pg=((2, 6, 16, 128), BF),
        lx=((2, 2, 8, 16, 128), BF),
        lg=((2, 2, 8, 16, 128), BF),
        pxt=((2, 3, 16, 256), BF),
        pgt=((2, 3, 16, 256), BF),
        lxt=((2, 2, 5, 16, 256), BF),
        lgt=((2, 2, 5, 16, 256), BF),
        terms=((4, 2, 2, 2, ROWS, 16, 256), BF),
        c_land=((4, 2, 2, ROWS, 16, 256), BF),
        u=((4, 2, 2, ROWS, 16, 256), BF),
        da=((3, 2, 2, ROWS, 16, 256), BF),
        db=((3, 4, ROWS, 16, 256), BF),
        va=((2, 2, ROWS, 16, 256), BF),
        vb=((4, ROWS, 16, 256), BF),
        ea=((3, ROWS, 16, 256), BF),
        eb=((3, ROWS, 16, 256), BF),
        dc=((2, 2, ROWS, 16, 256), BF),
        g=((2, 2, 2, ROWS, 16, 256), BF),
        zs=((8, 32, 256), BF),
        zr=((7, 32, 256), BF),
        zs1=((8, 32, 128), BF),
        zr1=((7, 32, 128), BF),
        fin=((128, 128), F32),
        local=dma((8,)),
        h_send=dma((4, 17)),
        h_recv=dma((4, 17)),
        rs_send=dma((2, 28)),
        rs_recv=dma((2, 28)),
    )


def base_conv(src, parts, weights, turned):
    blocks = []
    for t, h0, n in parts:
        blocks.append(jnp.concatenate(
            [src[t + a, pl.ds(h0 + b, n)].reshape(n * 32, 128) for a in range(3) for b in range(3)],
            axis=1,
        ))
    lhs = jnp.concatenate(blocks, axis=0) if len(blocks) > 1 else blocks[0]
    y = dot(lhs, weights, 1, 1 if turned else 0).reshape(-1, 32, 384)
    y = y[..., 128:256] + shift_cols(y[..., :128], 1) + shift_cols(y[..., 256:], -1)
    return y.reshape(-1, 128)


def kernel(comm, skip, scales, frames, kb, kd, kt, cot, feat, gf, out_base, out_down, out_top, *refs):
    names = list(scratch_list())
    s = SimpleNamespace(**dict(zip(names, refs)))
    if comm:
        where = (lax.axis_index("tm"), lax.axis_index("row"), lax.axis_index("col"))
    else:
        where = (jnp.int32(0), jnp.int32(0), jnp.int32(0))
    tm, row, col = where
    loads = [
        pltpu.make_async_copy(frames, s.xe.at[pl.ds(2, 4), pl.ds(1, 24)], s.local.at[0]),
        pltpu.make_async_copy(kb.at[:, 0], s.wf.at[:, :, pl.ds(0, 128)], s.local.at[1]),
        pltpu.make_async_copy(kb.at[:, 1], s.wf.at[:, :, pl.ds(128, 128)], s.local.at[2]),
        pltpu.make_async_copy(kb.at[:, 2], s.wf.at[:, :, pl.ds(256, 128)], s.local.at[3]),
        pltpu.make_async_copy(kd, s.kd, s.local.at[4]),
        pltpu.make_async_copy(kt, s.kt, s.local.at[5]),
        pltpu.make_async_copy(cot, s.cot, s.local.at[6]),
    ]
    for load in loads:
        load.start()
    halo_x = Halo(comm, s.xe, s.px, s.lx, s.h_send.at[0], s.h_recv.at[0], 4, 24, False, where)
    halo_xt = Halo(comm, s.xt.at[1], s.pxt, s.lxt, s.h_send.at[1], s.h_recv.at[1], 2, 12, False, where)
    halo_gt = Halo(comm, s.gt.at[1], s.pgt, s.lgt, s.h_send.at[2], s.h_recv.at[2], 2, 12, True, where)
    halo_g = Halo(comm, s.ge, s.pg, s.lg, s.h_send.at[3], s.h_recv.at[3], 4, 24, True, where)
    rs_top = Reduce(comm, s, 0, 0, TOP + 2, where)
    rs_low = Reduce(comm, s, 1, TOP + 2, ROWS - TOP - 2, where)

    if comm:
        barrier = pltpu.get_barrier_semaphore()
        near = [(a, b, c) for a in (0, 1, -1) for b in (0, 1, -1) for c in (0, 1, -1)][1:]
        far = [(2, 0, 0), (4, 0, 0), (6, 0, 0), (0, 2, 0)] + [(0, 0, d) for d in (2, 3, 4, 5, 6)]
        for dt, dh, dw in near + far:
            pl.semaphore_signal(
                barrier, inc=1,
                device_id=((tm + dt + 8) % 8, (row + dh + 4) % 4, (col + dw + 8) % 8),
                device_id_type=pl.DeviceIdType.MESH,
            )
    loads[0].wait()
    left, right = [], []
    for t in range(4):
        left.append(s.xe[2 + t, pl.ds(1, 24), pl.ds(0, 16)].astype(F32)[:, 0:1])
        right.append(s.xe[2 + t, pl.ds(1, 24), pl.ds(16, 16)].astype(F32)[:, 15:16])
    s.px[0] = pack(pick(left))
    s.px[1] = pack(pick(right))
    if comm:
        pl.semaphore_wait(barrier, len(near) + len(far))
    halo_x.start()

    for load in loads[1:4]:
        load.wait()
    for ab in range(9):
        for c in range(3):
            s.wb[c * 128:(c + 1) * 128, ab * 128:(ab + 1) * 128] = (
                s.wf[8 - ab, :, (2 - c) * 128:(3 - c) * 128])
    for load in loads[4:]:
        load.wait()

    def forward(*parts):
        value = base_conv(s.xe, parts, s.wf[...].reshape(1152, 384), False)
        at = 0
        for t, h0, n in parts:
            s.pre[t, h0 * 32:(h0 + n) * 32] = value[at:at + n * 32]
            at += n * 32

    if "fwd" not in skip:
        forward((2, 8, 8), (3, 8, 8))
        halo_x.wait(0)
        forward((2, 0, 8), (2, 16, 8))
        forward((3, 0, 8), (3, 16, 8))
        halo_x.wait(1)
        forward((0, 0, 24))
        forward((1, 0, 24))
        halo_x.wait(2)
    for side in range(2):
        column = halo_x.column(side)
        pieces = []
        for a in range(3):
            moved = pltpu.roll(column, 8 - a, 1) if a else column
            for b in range(3):
                pieces.append(moved[b:b + 24].reshape(192, 128).astype(BF))
        lhs = jnp.concatenate(pieces, axis=1)
        s.colx[side] = lhs
        c = 2 * side
        s.hl[side] = dot(lhs, s.wf[:, :, c * 128:(c + 1) * 128].reshape(1152, 128))
    for t in range(4):
        for side in range(2):
            at = pl.ds(31 * side, 24, stride=32)
            s.pre[t, at] = s.pre[t, at] + s.hl[side, pl.ds(t, 24, stride=8)]

    def act(i, _):
        t, h1 = i // 3, (i % 3) * 4
        rows = pl.ds(pl.multiple_of(h1 * 64, 256), 256)
        pre = s.pre[t, rows]
        q = logistic(pre)
        x = s.xe[2 + t, pl.ds(1 + 2 * h1, 8)].reshape(256, 128).astype(F32)
        hidden = (x + pre * q).astype(BF).astype(F32)
        s.hg[t, pl.ds(h1, 4)] = hidden.reshape(4, 2, 32, 128)
        s.pre[t, rows] = q * (1.0 + pre * (1.0 - q))
        return _

    lax.fori_loop(0, 12, act, 0)
    for t in range(4):
        for c in range(2):
            s.hc[c, t // 2, t % 2] = s.hg[t, :, :, pl.ds(c, 16, stride=2), :].astype(BF)
    taps = [(a, b, c) for a in range(2) for b in range(2) for c in range(2)]
    lhs = jnp.concatenate([s.hc[c, :, a, :, b].reshape(384, 128) for a, b, c in taps], axis=1)
    reduced = dot(lhs, s.kd[...]).astype(BF)
    red32 = reduced.astype(F32).reshape(2, 12, 16, 256)
    s.xt[1, pl.ds(2, 2), pl.ds(1, 12)] = reduced.reshape(2, 12, 16, 256)
    for side, w in ((0, 0), (1, 15)):
        s.pxt[side] = pack(pick([red32[t, :, w:w + 1] for t in range(2)]))
    halo_xt.start()

    for f in range(6):
        for b in range(3):
            s.xf[b, :, f * 768:(f + 1) * 768] = s.xe[f, pl.ds(b, 24)].reshape(768, 128).T
    for i, (a, b, c) in enumerate(taps):
        s.hf[i] = s.hc[c, :, a, :, b].reshape(384, 128).T

    def sides(halo, ext):
        for side in range(2):
            column = halo.column(side)
            for t in range(4):
                body = ext[1, t].astype(F32)
                rolled = pltpu.roll(body, 15 if side else 1, 1)
                edge = jnp.broadcast_to(column[:, t:t + 1], body.shape)
                put = jnp.where(iota(body.shape, 1) == (15 if side else 0), edge, rolled)
                ext[2 * side, t] = put.astype(BF)

    for kind in range(3):
        halo_xt.wait(kind)
    sides(halo_xt, s.xt)

    def top_conv(ext, turned):
        s.acc_t[...] = jnp.zeros((384, 256), F32)

        def step(ab, _):
            a, b = ab // 3, ab % 3
            lhs = jnp.concatenate(
                [ext[c, pl.ds(a, 2), pl.ds(b, 12)].reshape(384, 256) for c in range(3)], axis=1)
            if turned:
                rhs = jnp.concatenate([s.kt[26 - 3 * ab - c] for c in range(3)], axis=1)
                s.acc_t[...] += dot(lhs, rhs, 1, 1)
            else:
                s.acc_t[...] += dot(lhs, s.kt[pl.ds(3 * ab, 3)].reshape(768, 256))
            return _

        lax.fori_loop(0, 9, step, 0)
        return s.acc_t[...]

    if "top" not in skip:
        top_conv(s.xt, False)
    pre_top = s.acc_t[...]
    q = logistic(pre_top)
    red = s.xt[1, pl.ds(2, 2), pl.ds(1, 12)].reshape(384, 256).astype(F32)
    feat[...] = (red + pre_top * q).astype(BF)
    up = s.cot[...].astype(F32)
    slope = (up * (q * (1.0 + pre_top * (1.0 - q)))).astype(BF)
    s.grd[...] = slope
    slope32 = slope.astype(F32).reshape(2, 12, 16, 256)
    s.gt[1, pl.ds(0, 2), pl.ds(1, 12)] = slope.reshape(2, 12, 16, 256)
    for side, w in ((0, 0), (1, 15)):
        s.pgt[side] = pack(pick([slope32[t, :, w:w + 1] for t in range(2)]))
    halo_gt.start()

    def top_taps(abs_):
        lhs = jnp.concatenate(
            [s.xt[c, pl.ds(ab // 3, 2), pl.ds(ab % 3, 12)].reshape(384, 256)
             for ab in abs_ for c in range(3)], axis=1)
        return dot(lhs, s.grd[...], 0, 0).reshape(-1, 32, 8, 256)

    def top_store(r, first, second):
        both = jnp.concatenate([first, second], axis=1)
        s.terms[:, :, :, :, r] = both.astype(BF).reshape(4, 2, 2, 2, 16, 256)

    def top_six(i, _):
        group = top_taps([2 * i, 2 * i + 1])
        for k in range(3):
            top_store(3 * i + k, group[2 * k], group[2 * k + 1])
        return _

    if "tgrad" not in skip:
        lax.fori_loop(0, 4, top_six, 0)
    group = top_taps([8])
    top_store(12, group[0], group[1])
    top_store(13, group[2], jnp.zeros((32, 8, 256), F32))
    rs_top.start(0, TOP)

    for kind in range(3):
        halo_gt.wait(kind)
    sides(halo_gt, s.gt)
    if "top" not in skip:
        top_conv(s.gt, True)
    grad_red = (s.cot[...].astype(F32) + s.acc_t[...]).astype(BF)
    s.grd[...] = grad_red

    def store_low(r, lanes, group):
        first, second = weave(group[0], group[1]), weave(group[2], group[3])
        for par in range(2):
            both = jnp.concatenate([first[par], second[par]], axis=1).astype(BF)
            s.terms[:, :, :, par, r, :, lanes] = both.reshape(4, 2, 2, 16, both.shape[2])

    terms = dot(s.hf[...].reshape(1024, 384), s.grd[...]).reshape(8, 128, 256)
    for g in range(2):
        store_low(TOP + g, slice(0, 256), [terms[4 * g + i] for i in range(4)])
    rs_top.start(TOP, 2)

    spread = dot(grad_red, s.kd[...], 1, 1)
    for i, (a, b, c) in enumerate(taps):
        part = spread[:, i * 128:(i + 1) * 128].reshape(2, 12, 16, 128)
        for t in range(2):
            s.hg[2 * t + a, :, b, pl.ds(c, 16, stride=2), :] = part[t]

    low, high = [], []
    for t in range(4):
        gh = s.hg[t].reshape(24, 32, 128)
        slope = (gh * s.pre[t].reshape(24, 32, 128)).astype(BF)
        s.ge[t, pl.ds(1, 24)] = slope
        slope32 = slope.astype(F32)
        low.append(slope32[:, 0:1])
        high.append(slope32[:, 31:32])
        s.s3[t, :, 128:256] = slope.reshape(768, 128)
        s.s3[t, :, :128] = shift_cols(slope32, -1).astype(BF).reshape(768, 128)
        s.s3[t, :, 256:] = shift_cols(slope32, 1).astype(BF).reshape(768, 128)
    for side, parts in enumerate((low, high)):
        edge = pick(parts)
        s.pg[side] = pack(edge)
        s.sg[side] = edge.reshape(192, 128).astype(BF)
    halo_g.start()
    rs_top.planes()

    def base_taps(a):
        lhs = s.xf[:, :, a * 768:a * 768 + 3072].reshape(384, 3072)
        total = dot(lhs, s.s3[...].reshape(3072, 384))
        s.acc[3 * a:3 * a + 3] = total.reshape(3, 128, 384)

    if "bgrad" not in skip:
        base_taps(0)
    rs_top.relay()
    if "bgrad" not in skip:
        base_taps(1)
        base_taps(2)
    for side in range(2):
        extra = dot(s.colx[side], s.sg[side], 0, 0)
        lanes = slice(256 * side, 256 * side + 128)
        s.acc[:, :, lanes] = s.acc[:, :, lanes] + extra.reshape(9, 128, 128)
    for g in range(7):
        group = []
        for tap in range(4 * g, 4 * g + 4):
            if tap < 27:
                c = tap % 3
                group.append(s.acc[tap // 3, :, c * 128:(c + 1) * 128])
            else:
                group.append(jnp.zeros((128, 128), F32))
        store_low(TOP + 2 + g // 2, slice(128 * (g % 2), 128 * (g % 2) + 128), group)
    s.terms[:, :, :, :, ROWS - 1, :, 128:] = jnp.zeros((4, 2, 2, 2, 16, 128), BF)
    rs_low.start(TOP + 2, ROWS - TOP - 2)

    def backward(t):
        value = base_conv(s.ge, [(t, 0, 24)], s.wb[...], True)
        gf[t] = s.hg[t].reshape(768, 128) + value

    for kind in range(3):
        halo_g.wait(kind)
    if "bwd" not in skip:
        backward(0)
    rs_top.lines()
    rs_low.planes()
    if "bwd" not in skip:
        backward(1)
        backward(2)
    rs_low.lines()
    rs_top.depth()
    if "bwd" not in skip:
        backward(3)
    rs_low.depth()
    for side in range(2):
        column = halo_g.column(side)
        pieces = []
        for a in range(3):
            moved = pltpu.roll(column, 8 - a, 1) if a else column
            for b in range(3):
                pieces.append(moved[b:b + 24].reshape(192, 128).astype(BF))
        lhs = jnp.concatenate(pieces, axis=1)
        c = 2 * side
        s.hl[side] = dot(lhs, s.wb[c * 128:(c + 1) * 128, :], 1, 1)
    for t in range(4):
        for side in range(2):
            at = pl.ds(31 * side, 24, stride=32)
            gf[t, at] = gf[t, at] + s.hl[side, pl.ds(t, 24, stride=8)]
    rs_top.finish_top(out_top, out_down, scales[1])
    rs_low.finish_base(out_base, scales[0])
    for user in (halo_x, halo_xt, halo_gt, halo_g, rs_top, rs_low):
        user.done()


def call(comm, skip, scales, *args):
    scratch = [pltpu.VMEM(*v) if isinstance(v, tuple) else v for v in scratch_list().values()]
    vmem = pl.BlockSpec(memory_space=pltpu.VMEM)
    params = dict(collective_id=0, has_side_effects=True) if comm else {}
    return pl.pallas_call(
        functools.partial(kernel, comm, skip, scales),
        out_shape=(
            jax.ShapeDtypeStruct((384, 256), BF),
            jax.ShapeDtypeStruct((4, 768, 128), F32),
            jax.ShapeDtypeStruct((16, 4, 27), F32),
            jax.ShapeDtypeStruct((8, 4, 32), F32),
            jax.ShapeDtypeStruct((27, 8, 32), F32),
        ),
        in_specs=[pl.BlockSpec(memory_space=pl.ANY)] * 5,
        out_specs=(vmem,) * 5,
        scratch_shapes=scratch,
        compiler_params=pltpu.CompilerParams(vmem_limit_bytes=60 * 1024 * 1024, **params),
        cost_estimate=pl.CostEstimate(flops=13 * 10**9, bytes_accessed=10**7, transcendentals=10**6),
    )(*args)


def hand_over_kernel(*refs):
    n = (len(refs) - 2) // 3
    come, go = refs[-2:]
    pieces = []
    for src, dst, mid in zip(refs[:n], refs[n:2 * n], refs[2 * n:3 * n]):
        if src.shape[0] == 4:
            pieces += [(src.at[t], mid.at[t], dst.at[t]) for t in range(4)]
        else:
            pieces.append((src, mid, dst))
    inward = [pltpu.make_async_copy(a, b, come.at[i]) for i, (a, b, c) in enumerate(pieces)]
    outward = [pltpu.make_async_copy(b, c, go.at[i]) for i, (a, b, c) in enumerate(pieces)]
    for copy in inward:
        copy.start()
    for copy, after in zip(inward, outward):
        copy.wait()
        after.start()
    for copy in outward:
        copy.wait()


def hand_over(*arrays):
    n = len(arrays) + 3
    return pl.pallas_call(
        hand_over_kernel,
        out_shape=tuple(jax.ShapeDtypeStruct(a.shape, a.dtype) for a in arrays),
        in_specs=[pl.BlockSpec(memory_space=pl.ANY)] * len(arrays),
        out_specs=tuple(pl.BlockSpec(memory_space=pl.ANY) for _ in arrays),
        scratch_shapes=[pltpu.VMEM(a.shape, a.dtype) for a in arrays]
        + [pltpu.SemaphoreType.DMA((n,)), pltpu.SemaphoreType.DMA((n,))],
    )(*arrays)


def body(frames_in, kernel_base, kernel_down, kernel_top, cotangent, comm=True, skip=()):
    devices = 1
    if comm:
        devices = lax.axis_size("tm") * lax.axis_size("row") * lax.axis_size("col")
    scales = (1.0 / math.sqrt(devices * 3072), 1.0 / math.sqrt(devices * 384))
    feat, gf, base, down, top = call(
        comm, skip, scales,
        frames_in,
        kernel_base.reshape(9, 3, 128, 128),
        kernel_down.reshape(1024, 256),
        kernel_top.reshape(27, 256, 256),
        cotangent.reshape(384, 256),
    )
    gf, feat, base, down, top = hand_over(gf, feat, base, down, top)
    return (
        feat.reshape(2, 12, 16, 256),
        gf.reshape(4, 24, 32, 128),
        base.transpose(2, 0, 1),
        down.transpose(0, 2, 1),
        top.transpose(0, 2, 1),
    )


def solution(mesh):
    return jax.shard_map(
        body,
        mesh=mesh,
        in_specs=(P("tm", "row", "col", None), P(), P(), P(), P("tm", "row", "col", None)),
        out_specs=(
            P("tm", "row", "col", None),
            P("tm", "row", "col", None),
            P(None, "col", ("tm", "row")),
            P(None, "col", ("tm", "row")),
            P(None, "col", ("tm", "row")),
        ),
        check_vma=False,
    )
```

```python
import functools
import math
from types import SimpleNamespace

import jax
import jax.numpy as jnp
from jax import lax
from jax.experimental import pallas as pl
from jax.experimental.pallas import tpu as pltpu
from jax.sharding import PartitionSpec as P

F32 = jnp.float32
BF = jnp.bfloat16
ROWS = 20
TOP = 14


def dot(a, b, ca=1, cb=0):
    return lax.dot_general(a, b, (((ca,), (cb,)), ((), ())), preferred_element_type=F32)


def iota(shape, dim):
    return lax.broadcasted_iota(jnp.int32, shape, dim)


def shift_cols(value, by):
    width = value.shape[1]
    rolled = pltpu.roll(value, by % width, 1)
    gap = 0 if by > 0 else width - 1
    return jnp.where(iota(value.shape, 1) == gap, 0.0, rolled)


def pick(parts):
    out = jnp.zeros((parts[0].shape[0], 8, parts[0].shape[2]), F32)
    row = iota(out.shape, 1)
    for t, part in enumerate(parts):
        out = jnp.where(row == t, jnp.broadcast_to(part, out.shape), out)
    return out


def pack(value):
    h, _, c = value.shape
    pairs = value.reshape(h // 2, 2, 8, c)
    both = pairs[:, 0] + pltpu.roll(pairs[:, 1], 4, 1)
    return both.reshape(h // 4, 16, c).astype(BF)


def unpack_rows(groups, h):
    g, _, c = groups.shape
    pairs = groups.astype(F32).reshape(2 * g, 8, c)
    low = iota(pairs.shape, 1) < 4
    even = jnp.where(low, pairs, 0.0)
    odd = jnp.where(low, pltpu.roll(pairs, 4, 1), 0.0)
    rows = jnp.stack([even, odd], axis=1).reshape(4 * g, 8, c)
    return rows[3:h + 5]


def logistic(s):
    return 1.0 / (1.0 + jnp.exp(-s))


def weave(first, second):
    first = first.reshape(16, 8, first.shape[1])
    second = second.reshape(16, 8, second.shape[1])
    low = iota(first.shape, 1) < 4
    even = jnp.where(low, first, pltpu.roll(second, 4, 1))
    odd = jnp.where(low, pltpu.roll(first, 4, 1), second)
    return even, odd


class Halo:
    def __init__(self, comm, body, cols, land, send, recv, frames, height, back, where):
        self.comm, self.body, self.cols, self.land = comm, body, cols, land
        self.send, self.recv, self.back = send, recv, back
        self.frames, self.height, self.where = frames, height, where
        self.own = 0 if back else 2
        self.copies = []

    def start(self):
        tm, row, col = self.where
        step = -1 if self.back else 1
        h, f, own, body = self.height, self.frames, self.own, self.body
        edge = 0 if self.back else own + f - 2
        into = f if self.back else 0
        jobs = []
        for dt in (0, step):
            first, count, put = (own, f, own) if dt == 0 else (edge, 2, into)
            kind = 0 if dt == 0 else 1
            for dh in (0, 1, -1):
                src_h, n, dst_h = {0: (1, h, 1), 1: (h, 1, 0), -1: (1, 1, h + 1)}[dh]
                if dt or dh:
                    jobs.append((kind, (dt, dh, 0),
                                 body.at[pl.ds(first, count), pl.ds(src_h, n)],
                                 body.at[pl.ds(put, count), pl.ds(dst_h, n)]))
                g = h // 4
                src_g, n_g, dst_g = {0: (0, g, 1), 1: (g - 1, 1, 0), -1: (0, 1, g + 1)}[dh]
                for dw in (1, -1):
                    side = 0 if dw == 1 else 1
                    jobs.append((2, (dt, dh, dw),
                                 self.cols.at[1 - side, pl.ds(src_g, n_g)],
                                 self.land.at[side, kind, pl.ds(dst_g, n_g)]))
        jobs.sort(key=lambda job: job[0])
        if not self.comm:
            return
        for i, (kind, (dt, dh, dw), src, dst) in enumerate(jobs):
            copy = pltpu.make_async_remote_copy(
                src_ref=src, dst_ref=dst, send_sem=self.send.at[i], recv_sem=self.recv.at[i],
                device_id=((tm + dt + 8) % 8, (row + dh + 4) % 4, (col + dw + 8) % 8),
                device_id_type=pl.DeviceIdType.MESH,
            )
            copy.start()
            self.copies.append((kind, copy))

    def wait(self, kind):
        for k, copy in self.copies:
            if k == kind:
                copy.wait_recv()
        row = self.where[1]
        zero = jnp.zeros(self.body.shape[2:], BF)
        frames = range(self.own, self.own + self.frames)
        if kind == 1:
            first = self.frames if self.back else 0
            frames = range(first, first + 2)

            @pl.when(self.where[0] == (7 if self.back else 0))
            def _():
                for t in frames:
                    for r in range(self.height + 2):
                        self.body[t, r] = zero

        if kind < 2:
            @pl.when(row == 0)
            def _():
                for t in frames:
                    self.body[t, 0] = zero

            @pl.when(row == 3)
            def _():
                for t in frames:
                    self.body[t, self.height + 1] = zero

    def column(self, side):
        tm, row, col = self.where
        cur = unpack_rows(self.land[side, 0], self.height)
        far = unpack_rows(self.land[side, 1], self.height)
        shape = cur.shape
        at_t, at_h = iota(shape, 1), iota(shape, 0)
        out = col == (7 if side else 0)
        edge = tm == (7 if self.back else 0)
        if self.back:
            is_far = at_t >= self.frames
            far = pltpu.roll(far, self.frames, 1)
        else:
            is_far = at_t < 2
            far = pltpu.roll(far, 8 - (self.frames - 2), 1) if self.frames > 2 else far
            cur = pltpu.roll(cur, 2, 1)
        drop = ((at_h == 0) & (row == 0)) | ((at_h == shape[0] - 1) & (row == 3))
        drop = drop | out | (is_far & edge) | (at_t >= self.frames + 2)
        return jnp.where(drop, 0.0, jnp.where(is_far, far, cur))

    def done(self):
        for _, copy in self.copies:
            copy.wait_send()


class Reduce:
    def __init__(self, comm, s, job, r0, n, first, where):
        self.comm, self.s, self.job, self.r0, self.n = comm, s, job, r0, n
        self.first = first
        tm, row, col = where
        self.y, self.core, self.x, self.z = tm // 2, tm % 2, row, col
        self.started = []
        self.pending = {}
        self.slot = 0

    def put(self, key, src, dst, y, core, x, z):
        if not self.comm:
            return
        i = self.slot
        self.slot += 1
        copy = pltpu.make_async_remote_copy(
            src_ref=src, dst_ref=dst,
            send_sem=self.s.rs_send.at[self.job, i], recv_sem=self.s.rs_recv.at[self.job, i],
            device_id=(2 * y + core, x, z), device_id_type=pl.DeviceIdType.MESH,
        )
        copy.start()
        self.started.append(copy)
        self.pending.setdefault(key, []).append(copy)

    def arrive(self, key):
        for copy in self.pending.pop(key, []):
            copy.wait_recv()

    def a(self):
        return pl.ds(self.r0, self.first)

    def b(self):
        return pl.ds(self.r0 + self.first, self.n - self.first)

    def halves(self, part):
        r0, n = (self.r0, self.first) if part == "a" else (self.r0 + self.first, self.n - self.first)
        return pl.ds(r0, n // 2), pl.ds(r0 + n // 2, n // 2)

    def start(self, key, r0, n):
        r = pl.ds(r0, n)
        self.put("core" + key, self.s.terms.at[:, 1 - self.core, :, :, r],
                 self.s.c_land.at[:, :, :, r], self.y, 1 - self.core, self.x, self.z)

    def fold(self, key, r):
        s = self.s
        self.arrive("core" + key)

        def add(i, _):
            yy, x1, par = i // 4, (i % 4) // 2, i % 2
            s.u[yy, x1, par, r] = (
                s.terms[yy, self.core, x1, par, r].astype(F32) + s.c_land[yy, x1, par, r].astype(F32)
            ).astype(BF)
            return _

        lax.fori_loop(0, 16, add, 0)

    def along(self, key, part, step, unit, r, land):
        s = self.s
        if part == "a":
            to, unit = (self.y + step) % 4, (self.y + unit) % 4
            self.put(key, s.u.at[unit, :, :, r], s.da.at[land, :, :, r],
                     to, self.core, self.x, self.z)
        else:
            to, unit = (self.x + step) % 4, (self.x + unit) % 4
            self.put(key, s.u.at[:, unit // 2, unit % 2, r], s.db.at[land, :, r],
                     self.y, self.core, to, self.z)

    def send(self, part):
        self.fold(part, self.a() if part == "a" else self.b())
        p, q = self.halves(part)
        self.along("relay" + part, part, 1, 2, p, 0)
        self.along("relay" + part, part, 3, 2, q, 0)
        self.along("line" + part, part, 1, 1, q, 1)
        self.along("line" + part, part, 3, 3, p, 1)

    def relay(self, part):
        s, y, x = self.s, self.y, self.x
        self.arrive("relay" + part)
        p, q = self.halves(part)
        if part == "a":
            up, down = (y + 1) % 4, (y + 3) % 4
        else:
            up, down = (x + 1) % 4, (x + 3) % 4

        def add(i, _):
            x1, par = i // 2, i % 2
            for to, r in ((up, p), (down, q)):
                if part == "a":
                    s.g[0, x1, par, r] = (
                        s.u[to, x1, par, r].astype(F32) + s.da[0, x1, par, r].astype(F32)).astype(BF)
                else:
                    s.g[1, x1, par, r] = (
                        s.u[i, to // 2, to % 2, r].astype(F32) + s.db[0, i, r].astype(F32)).astype(BF)
            return _

        lax.fori_loop(0, 4, add, 0)
        for to, r in ((up, p), (down, q)):
            if part == "a":
                self.put("linea", s.g.at[0, :, :, r], s.da.at[2, :, :, r],
                         to, self.core, x, self.z)
            else:
                self.put("lineb", s.g.at[1, :, :, r], s.dc.at[:, :, r],
                         y, self.core, to, self.z)

    def planes(self):
        for part in ("a", "b"):
            self.fold(part, self.a() if part == "a" else self.b())
            for d in (2, 1, 3):
                self.along("line" + part, part, d, d, self.a() if part == "a" else self.b(), d - 1)

    def lines(self, part):
        s, y, x = self.s, self.y, self.x
        self.arrive("line" + part)

        def add(i, _):
            x1, par = i // 2, i % 2
            if part == "a":
                total = s.u[y, x1, par, self.a()].astype(F32)
                for d in range(1 if self.job == 0 else 0, 3):
                    total = total + s.da[d, x1, par, self.a()].astype(F32)
                s.va[x1, par, self.a()] = total.astype(BF)
                return _
            total = s.u[i, x // 2, x % 2, self.b()].astype(F32)
            if self.job == 0:
                total = total + s.db[1, i, self.b()].astype(F32)
                total = total + s.dc[x1, par, self.b()].astype(F32)
            else:
                for d in range(3):
                    total = total + s.db[d, i, self.b()].astype(F32)
            s.vb[i, self.b()] = total.astype(BF)
            return _

        lax.fori_loop(0, 4, add, 0)
        for d in (2, 1, 3):
            if part == "a":
                to = (x + d) % 4
                self.put("depth", s.va.at[to // 2, to % 2, self.a()], s.ea.at[d - 1, self.a()],
                         y, self.core, to, self.z)
            else:
                to = (y + d) % 4
                self.put("depth", s.vb.at[to, self.b()], s.eb.at[d - 1, self.b()],
                         to, self.core, x, self.z)

    def depth(self):
        s, y, x = self.s, self.y, self.x
        self.arrive("depth")
        first = s.va[x // 2, x % 2, self.a()].astype(F32)
        second = s.vb[y, self.b()].astype(F32)
        for d in range(3):
            first = first + s.ea[d, self.a()].astype(F32)
            second = second + s.eb[d, self.b()].astype(F32)
        both = jnp.concatenate([first.reshape(-1, 256), second.reshape(-1, 256)], axis=0)
        if self.job == 0:
            s.zs[...] = both.T.astype(BF).reshape(8, 32, 256)
            src, dst = s.zs, s.zr
        else:
            base = jnp.concatenate([both, jnp.zeros((64, 256), F32)], axis=0).T
            s.zs1[:, :16] = base[:128].astype(BF).reshape(8, 16, 128)
            s.zs1[:, 16:] = base[128:].astype(BF).reshape(8, 16, 128)
            src, dst = s.zs1, s.zr1
        for d in (4, 3, 5, 2, 6, 1, 7):
            to = (self.z + d) % 8
            self.put("z", src.at[to], dst.at[d - 1], y, self.core, x, to)

    def total(self):
        s = self.s
        self.arrive("z")
        src, dst = (s.zs, s.zr) if self.job == 0 else (s.zs1, s.zr1)
        total = src[self.z].astype(F32)
        if self.comm:
            for d in range(7):
                total = total + dst[d].astype(F32)
        pad = jnp.zeros((96, total.shape[1]), F32)
        return jnp.concatenate([total, pad], axis=0)

    def finish_top(self, top, down, scale):
        turned = self.total().T * scale
        top[...] = turned[:216, :32].reshape(27, 8, 32)
        for tap in range(8):
            down[tap] = turned[224 + 4 * tap:228 + 4 * tap, :32]

    def finish_base(self, out, scale):
        s = self.s
        s.fin[...] = self.total().T * scale
        parts = []
        low = iota((8, 128), 0) < 4
        for k in range(4):
            rows = s.fin[pl.ds(k, 16, stride=4), :]
            beside = pltpu.roll(rows, 112, 1)
            for j in range(2):
                first, second = rows[8 * j:8 * j + 8], beside[8 * j:8 * j + 8]
                parts.append(jnp.where(low, first, pltpu.roll(second, 4, 0)))
                parts.append(jnp.where(low, pltpu.roll(first, 4, 0), second))
        taps = jnp.concatenate(parts, axis=0).T[:16]
        for k in range(4):
            out[:, k, :] = (pltpu.roll(taps, 128 - 32 * k, 1) if k else taps)[:, :27]

    def done(self):
        for copy in self.started:
            copy.wait_send()


def scratch_list():
    dma = pltpu.SemaphoreType.DMA
    return dict(
        xe=((6, 26, 32, 128), BF),
        ge=((6, 26, 32, 128), BF),
        wf=((9, 128, 384), BF),
        wb=((384, 1152), BF),
        kd=((1024, 256), BF),
        kt=((27, 256, 256), BF),
        cot=((384, 256), BF),
        pre=((4, 768, 128), F32),
        hg=((4, 12, 2, 32, 128), F32),
        hc=((2, 2, 2, 12, 2, 16, 128), BF),
        s3=((4, 768, 384), BF),
        colx=((2, 192, 1152), BF),
        hl=((2, 192, 128), F32),
        acc=((9, 128, 384), F32),
        xf=((3, 128, 4608), BF),
        hf=((8, 128, 384), BF),
        xt=((3, 4, 14, 16, 256), BF),
        gt=((3, 4, 14, 16, 256), BF),
        acc_t=((384, 256), F32),
        grd=((384, 256), BF),
        sg=((2, 192, 128), BF),
        px=((2, 6, 16, 128), BF),
        pg=((2, 6, 16, 128), BF),
        lx=((2, 2, 8, 16, 128), BF),
        lg=((2, 2, 8, 16, 128), BF),
        pxt=((2, 3, 16, 256), BF),
        pgt=((2, 3, 16, 256), BF),
        lxt=((2, 2, 5, 16, 256), BF),
        lgt=((2, 2, 5, 16, 256), BF),
        terms=((4, 2, 2, 2, ROWS, 16, 256), BF),
        c_land=((4, 2, 2, ROWS, 16, 256), BF),
        u=((4, 2, 2, ROWS, 16, 256), BF),
        da=((3, 2, 2, ROWS, 16, 256), BF),
        db=((3, 4, ROWS, 16, 256), BF),
        va=((2, 2, ROWS, 16, 256), BF),
        vb=((4, ROWS, 16, 256), BF),
        ea=((3, ROWS, 16, 256), BF),
        eb=((3, ROWS, 16, 256), BF),
        dc=((2, 2, ROWS, 16, 256), BF),
        g=((2, 2, 2, ROWS, 16, 256), BF),
        zs=((8, 32, 256), BF),
        zr=((7, 32, 256), BF),
        zs1=((8, 32, 128), BF),
        zr1=((7, 32, 128), BF),
        fin=((128, 128), F32),
        gfs=((4, 768, 128), F32),
        feats=((384, 256), BF),
        leave=dma((5,)),
        local=dma((8,)),
        h_send=dma((4, 17)),
        h_recv=dma((4, 17)),
        rs_send=dma((2, 28)),
        rs_recv=dma((2, 28)),
    )


def base_conv(src, parts, weights, turned):
    blocks = []
    for t, h0, n in parts:
        blocks.append(jnp.concatenate(
            [src[t + a, pl.ds(h0 + b, n)].reshape(n * 32, 128) for a in range(3) for b in range(3)],
            axis=1,
        ))
    lhs = jnp.concatenate(blocks, axis=0) if len(blocks) > 1 else blocks[0]
    y = dot(lhs, weights, 1, 1 if turned else 0).reshape(-1, 32, 384)
    y = y[..., 128:256] + shift_cols(y[..., :128], 1) + shift_cols(y[..., 256:], -1)
    return y.reshape(-1, 128)


def kernel(comm, skip, scales, frames, kb, kd, kt, cot, feat, gf, out_base, out_down, out_top, *refs):
    names = list(scratch_list())
    s = SimpleNamespace(**dict(zip(names, refs)))
    if comm:
        where = (lax.axis_index("tm"), lax.axis_index("row"), lax.axis_index("col"))
    else:
        where = (jnp.int32(0), jnp.int32(0), jnp.int32(0))
    tm, row, col = where
    loads = [
        pltpu.make_async_copy(frames, s.xe.at[pl.ds(2, 4), pl.ds(1, 24)], s.local.at[0]),
        pltpu.make_async_copy(kb.at[:, 0], s.wf.at[:, :, pl.ds(0, 128)], s.local.at[1]),
        pltpu.make_async_copy(kb.at[:, 1], s.wf.at[:, :, pl.ds(128, 128)], s.local.at[2]),
        pltpu.make_async_copy(kb.at[:, 2], s.wf.at[:, :, pl.ds(256, 128)], s.local.at[3]),
        pltpu.make_async_copy(kd, s.kd, s.local.at[4]),
        pltpu.make_async_copy(kt, s.kt, s.local.at[5]),
        pltpu.make_async_copy(cot, s.cot, s.local.at[6]),
    ]
    for load in loads:
        load.start()
    halo_x = Halo(comm, s.xe, s.px, s.lx, s.h_send.at[0], s.h_recv.at[0], 4, 24, False, where)
    halo_xt = Halo(comm, s.xt.at[1], s.pxt, s.lxt, s.h_send.at[1], s.h_recv.at[1], 2, 12, False, where)
    halo_gt = Halo(comm, s.gt.at[1], s.pgt, s.lgt, s.h_send.at[2], s.h_recv.at[2], 2, 12, True, where)
    halo_g = Halo(comm, s.ge, s.pg, s.lg, s.h_send.at[3], s.h_recv.at[3], 4, 24, True, where)
    rs_top = Reduce(comm, s, 0, 0, TOP + 2, 10, where)
    rs_low = Reduce(comm, s, 1, TOP + 2, ROWS - TOP - 2, 2, where)

    if comm:
        barrier = pltpu.get_barrier_semaphore()
        near = [(a, b, c) for a in (0, 1, -1) for b in (0, 1, -1) for c in (0, 1, -1)][1:]
        far = [(2, 0, 0), (4, 0, 0), (6, 0, 0), (0, 2, 0)] + [(0, 0, d) for d in (2, 3, 4, 5, 6)]
        for dt, dh, dw in near + far:
            pl.semaphore_signal(
                barrier, inc=1,
                device_id=((tm + dt + 8) % 8, (row + dh + 4) % 4, (col + dw + 8) % 8),
                device_id_type=pl.DeviceIdType.MESH,
            )
    loads[0].wait()
    left, right = [], []
    for t in range(4):
        left.append(s.xe[2 + t, pl.ds(1, 24), pl.ds(0, 16)].astype(F32)[:, 0:1])
        right.append(s.xe[2 + t, pl.ds(1, 24), pl.ds(16, 16)].astype(F32)[:, 15:16])
    s.px[0] = pack(pick(left))
    s.px[1] = pack(pick(right))
    if comm:
        pl.semaphore_wait(barrier, len(near) + len(far))
    halo_x.start()

    for load in loads[1:4]:
        load.wait()
    for ab in range(9):
        for c in range(3):
            s.wb[c * 128:(c + 1) * 128, ab * 128:(ab + 1) * 128] = (
                s.wf[8 - ab, :, (2 - c) * 128:(3 - c) * 128])
    for load in loads[4:]:
        load.wait()

    def forward(*parts):
        value = base_conv(s.xe, parts, s.wf[...].reshape(1152, 384), False)
        at = 0
        for t, h0, n in parts:
            s.pre[t, h0 * 32:(h0 + n) * 32] = value[at:at + n * 32]
            at += n * 32

    if "fwd" not in skip:
        forward((2, 8, 8), (3, 8, 8))
        halo_x.wait(0)
        forward((2, 0, 8), (2, 16, 8))
        forward((3, 0, 8), (3, 16, 8))
        halo_x.wait(1)
        forward((0, 0, 24))
        forward((1, 0, 24))
        halo_x.wait(2)
    for side in range(2):
        column = halo_x.column(side)
        pieces = []
        for a in range(3):
            moved = pltpu.roll(column, 8 - a, 1) if a else column
            for b in range(3):
                pieces.append(moved[b:b + 24].reshape(192, 128).astype(BF))
        lhs = jnp.concatenate(pieces, axis=1)
        s.colx[side] = lhs
        c = 2 * side
        s.hl[side] = dot(lhs, s.wf[:, :, c * 128:(c + 1) * 128].reshape(1152, 128))
    for t in range(4):
        for side in range(2):
            at = pl.ds(31 * side, 24, stride=32)
            s.pre[t, at] = s.pre[t, at] + s.hl[side, pl.ds(t, 24, stride=8)]

    def act(i, _):
        t, h1 = i // 3, (i % 3) * 4
        rows = pl.ds(pl.multiple_of(h1 * 64, 256), 256)
        pre = s.pre[t, rows]
        q = logistic(pre)
        x = s.xe[2 + t, pl.ds(1 + 2 * h1, 8)].reshape(256, 128).astype(F32)
        hidden = (x + pre * q).astype(BF).astype(F32)
        s.hg[t, pl.ds(h1, 4)] = hidden.reshape(4, 2, 32, 128)
        return _

    lax.fori_loop(0, 12, act, 0)
    for t in range(4):
        for c in range(2):
            s.hc[c, t // 2, t % 2] = s.hg[t, :, :, pl.ds(c, 16, stride=2), :].astype(BF)
    taps = [(a, b, c) for a in range(2) for b in range(2) for c in range(2)]
    lhs = jnp.concatenate([s.hc[c, :, a, :, b].reshape(384, 128) for a, b, c in taps], axis=1)
    reduced = dot(lhs, s.kd[...]).astype(BF)
    red32 = reduced.astype(F32).reshape(2, 12, 16, 256)
    s.xt[1, pl.ds(2, 2), pl.ds(1, 12)] = reduced.reshape(2, 12, 16, 256)
    for side, w in ((0, 0), (1, 15)):
        s.pxt[side] = pack(pick([red32[t, :, w:w + 1] for t in range(2)]))
    halo_xt.start()

    def steep(i, _):
        t, h1 = i // 3, (i % 3) * 4
        rows = pl.ds(pl.multiple_of(h1 * 64, 256), 256)
        pre = s.pre[t, rows]
        q = logistic(pre)
        s.pre[t, rows] = q * (1.0 + pre * (1.0 - q))
        return _

    lax.fori_loop(0, 12, steep, 0)
    for f in range(6):
        for b in range(3):
            s.xf[b, :, f * 768:(f + 1) * 768] = s.xe[f, pl.ds(b, 24)].reshape(768, 128).T
    for i, (a, b, c) in enumerate(taps):
        s.hf[i] = s.hc[c, :, a, :, b].reshape(384, 128).T

    def sides(halo, ext):
        for side in range(2):
            column = halo.column(side)
            for t in range(4):
                body = ext[1, t].astype(F32)
                rolled = pltpu.roll(body, 15 if side else 1, 1)
                edge = jnp.broadcast_to(column[:, t:t + 1], body.shape)
                put = jnp.where(iota(body.shape, 1) == (15 if side else 0), edge, rolled)
                ext[2 * side, t] = put.astype(BF)

    for kind in range(3):
        halo_xt.wait(kind)
    sides(halo_xt, s.xt)

    def top_conv(ext, turned):
        for t in range(2):
            lhs = jnp.concatenate(
                [ext[c, a + t, b:b + 12].reshape(192, 256)
                 for a in range(3) for b in range(3) for c in range(3)], axis=1)
            if turned:
                rhs = jnp.concatenate([s.kt[26 - i] for i in range(27)], axis=1)
                part = dot(lhs, rhs, 1, 1)
            else:
                part = dot(lhs, s.kt[...].reshape(6912, 256))
            s.acc_t[192 * t:192 * t + 192] = part

    if "top" not in skip:
        top_conv(s.xt, False)
    pre_top = s.acc_t[...]
    q = logistic(pre_top)
    red = s.xt[1, pl.ds(2, 2), pl.ds(1, 12)].reshape(384, 256).astype(F32)
    s.feats[...] = (red + pre_top * q).astype(BF)
    leaving = [pltpu.make_async_copy(s.feats, feat, s.leave.at[4])]
    leaving[0].start()
    up = s.cot[...].astype(F32)
    slope = (up * (q * (1.0 + pre_top * (1.0 - q)))).astype(BF)
    s.grd[...] = slope
    slope32 = slope.astype(F32).reshape(2, 12, 16, 256)
    s.gt[1, pl.ds(0, 2), pl.ds(1, 12)] = slope.reshape(2, 12, 16, 256)
    for side, w in ((0, 0), (1, 15)):
        s.pgt[side] = pack(pick([slope32[t, :, w:w + 1] for t in range(2)]))
    halo_gt.start()

    def top_taps(abs_):
        lhs = jnp.concatenate(
            [s.xt[c, pl.ds(ab // 3, 2), pl.ds(ab % 3, 12)].reshape(384, 256)
             for ab in abs_ for c in range(3)], axis=1)
        return dot(lhs, s.grd[...], 0, 0).reshape(-1, 32, 8, 256)

    def top_store(r, first, second):
        both = jnp.concatenate([first, second], axis=1)
        s.terms[:, :, :, :, r] = both.astype(BF).reshape(4, 2, 2, 2, 16, 256)

    def top_six(i, _):
        group = top_taps([2 * i, 2 * i + 1])
        for k in range(3):
            top_store(3 * i + k, group[2 * k], group[2 * k + 1])
        return _

    if "tgrad" not in skip:
        lax.fori_loop(0, 4, top_six, 0)
    rs_top.start("a", 0, 10)
    group = top_taps([8])
    top_store(12, group[0], group[1])
    top_store(13, group[2], jnp.zeros((32, 8, 256), F32))
    rs_top.start("b", 10, TOP - 10)

    for kind in range(3):
        halo_gt.wait(kind)
    sides(halo_gt, s.gt)
    if "top" not in skip:
        top_conv(s.gt, True)
    rs_top.send("a")
    grad_red = (s.cot[...].astype(F32) + s.acc_t[...]).astype(BF)
    s.grd[...] = grad_red

    def store_low(r, lanes, group):
        first, second = weave(group[0], group[1]), weave(group[2], group[3])
        for par in range(2):
            both = jnp.concatenate([first[par], second[par]], axis=1).astype(BF)
            s.terms[:, :, :, par, r, :, lanes] = both.reshape(4, 2, 2, 16, both.shape[2])

    terms = dot(s.hf[...].reshape(1024, 384), s.grd[...]).reshape(8, 128, 256)
    for g in range(2):
        store_low(TOP + g, slice(0, 256), [terms[4 * g + i] for i in range(4)])
    rs_top.start("b", TOP, 2)

    spread = dot(grad_red, s.kd[...], 1, 1)
    for i, (a, b, c) in enumerate(taps):
        part = spread[:, i * 128:(i + 1) * 128].reshape(2, 12, 16, 128)
        for t in range(2):
            s.hg[2 * t + a, :, b, pl.ds(c, 16, stride=2), :] = part[t]

    low, high = [], []
    for t in range(4):
        gh = s.hg[t].reshape(24, 32, 128)
        slope = (gh * s.pre[t].reshape(24, 32, 128)).astype(BF)
        s.ge[t, pl.ds(1, 24)] = slope
        slope32 = slope.astype(F32)
        low.append(slope32[:, 0:1])
        high.append(slope32[:, 31:32])
        s.s3[t, :, 128:256] = slope.reshape(768, 128)
        s.s3[t, :, :128] = shift_cols(slope32, -1).astype(BF).reshape(768, 128)
        s.s3[t, :, 256:] = shift_cols(slope32, 1).astype(BF).reshape(768, 128)
    for side, parts in enumerate((low, high)):
        edge = pick(parts)
        s.pg[side] = pack(edge)
        s.sg[side] = edge.reshape(192, 128).astype(BF)
    halo_g.start()
    rs_top.send("b")

    def base_taps(a):
        lhs = s.xf[:, :, a * 768:a * 768 + 3072].reshape(384, 3072)
        total = dot(lhs, s.s3[...].reshape(3072, 384))
        s.acc[3 * a:3 * a + 3] = total.reshape(3, 128, 384)

    if "bgrad" not in skip:
        base_taps(0)
    rs_top.relay("a")
    if "bgrad" not in skip:
        base_taps(1)
        base_taps(2)
    rs_top.relay("b")
    for side in range(2):
        extra = dot(s.colx[side], s.sg[side], 0, 0)
        lanes = slice(256 * side, 256 * side + 128)
        s.acc[:, :, lanes] = s.acc[:, :, lanes] + extra.reshape(9, 128, 128)
    for g in range(7):
        group = []
        for tap in range(4 * g, 4 * g + 4):
            if tap < 27:
                c = tap % 3
                group.append(s.acc[tap // 3, :, c * 128:(c + 1) * 128])
            else:
                group.append(jnp.zeros((128, 128), F32))
        store_low(TOP + 2 + g // 2, slice(128 * (g % 2), 128 * (g % 2) + 128), group)
    s.terms[:, :, :, :, ROWS - 1, :, 128:] = jnp.zeros((4, 2, 2, 2, 16, 128), BF)
    rs_low.start("a", TOP + 2, ROWS - TOP - 2)
    rs_top.lines("a")

    for kind in range(3):
        halo_g.wait(kind)
    for side in range(2):
        column = halo_g.column(side)
        pieces = []
        for a in range(3):
            moved = pltpu.roll(column, 8 - a, 1) if a else column
            for b in range(3):
                pieces.append(moved[b:b + 24].reshape(192, 128).astype(BF))
        lhs = jnp.concatenate(pieces, axis=1)
        c = 2 * side
        s.hl[side] = dot(lhs, s.wb[c * 128:(c + 1) * 128, :], 1, 1)

    def backward(t):
        value = base_conv(s.ge, [(t, 0, 24)], s.wb[...], True)
        s.gfs[t] = s.hg[t].reshape(768, 128) + value
        for side in range(2):
            at = pl.ds(31 * side, 24, stride=32)
            s.gfs[t, at] = s.gfs[t, at] + s.hl[side, pl.ds(t, 24, stride=8)]
        copy = pltpu.make_async_copy(s.gfs.at[t], gf.at[t], s.leave.at[t])
        copy.start()
        leaving.append(copy)

    backward(0)
    rs_low.planes()
    rs_top.lines("b")
    backward(1)
    backward(2)
    rs_low.lines("a")
    rs_low.lines("b")
    backward(3)
    rs_top.depth()
    rs_low.depth()
    rs_top.finish_top(out_top, out_down, scales[1])
    rs_low.finish_base(out_base, scales[0])
    for copy in leaving:
        copy.wait()
    for user in (halo_x, halo_xt, halo_gt, halo_g, rs_top, rs_low):
        user.done()


def call(comm, skip, scales, *args):
    scratch = [pltpu.VMEM(*v) if isinstance(v, tuple) else v for v in scratch_list().values()]
    vmem = pl.BlockSpec(memory_space=pltpu.VMEM)
    params = dict(collective_id=0, has_side_effects=True) if comm else {}
    return pl.pallas_call(
        functools.partial(kernel, comm, skip, scales),
        out_shape=(
            jax.ShapeDtypeStruct((384, 256), BF),
            jax.ShapeDtypeStruct((4, 768, 128), F32),
            jax.ShapeDtypeStruct((16, 4, 27), F32),
            jax.ShapeDtypeStruct((8, 4, 32), F32),
            jax.ShapeDtypeStruct((27, 8, 32), F32),
        ),
        in_specs=[pl.BlockSpec(memory_space=pl.ANY)] * 5,
        out_specs=(pl.BlockSpec(memory_space=pl.ANY),) * 2 + (vmem,) * 3,
        scratch_shapes=scratch,
        compiler_params=pltpu.CompilerParams(vmem_limit_bytes=60 * 1024 * 1024, **params),
        cost_estimate=pl.CostEstimate(flops=13 * 10**9, bytes_accessed=10**7, transcendentals=10**6),
    )(*args)


def hand_over_kernel(*refs):
    n = (len(refs) - 2) // 3
    come, go = refs[-2:]
    pieces = []
    for src, dst, mid in zip(refs[:n], refs[n:2 * n], refs[2 * n:3 * n]):
        if src.shape[0] == 4:
            pieces += [(src.at[t], mid.at[t], dst.at[t]) for t in range(4)]
        else:
            pieces.append((src, mid, dst))
    inward = [pltpu.make_async_copy(a, b, come.at[i]) for i, (a, b, c) in enumerate(pieces)]
    outward = [pltpu.make_async_copy(b, c, go.at[i]) for i, (a, b, c) in enumerate(pieces)]
    for copy in inward:
        copy.start()
    for copy, after in zip(inward, outward):
        copy.wait()
        after.start()
    for copy in outward:
        copy.wait()


def hand_over(*arrays):
    n = len(arrays) + 3
    return pl.pallas_call(
        hand_over_kernel,
        out_shape=tuple(jax.ShapeDtypeStruct(a.shape, a.dtype) for a in arrays),
        in_specs=[pl.BlockSpec(memory_space=pl.ANY)] * len(arrays),
        out_specs=tuple(pl.BlockSpec(memory_space=pl.ANY) for _ in arrays),
        scratch_shapes=[pltpu.VMEM(a.shape, a.dtype) for a in arrays]
        + [pltpu.SemaphoreType.DMA((n,)), pltpu.SemaphoreType.DMA((n,))],
    )(*arrays)


def body(frames_in, kernel_base, kernel_down, kernel_top, cotangent, comm=True, skip=()):
    devices = 1
    if comm:
        devices = lax.axis_size("tm") * lax.axis_size("row") * lax.axis_size("col")
    scales = (1.0 / math.sqrt(devices * 3072), 1.0 / math.sqrt(devices * 384))
    feat, gf, base, down, top = call(
        comm, skip, scales,
        frames_in,
        kernel_base.reshape(9, 3, 128, 128),
        kernel_down.reshape(1024, 256),
        kernel_top.reshape(27, 256, 256),
        cotangent.reshape(384, 256),
    )
    gf, feat, base, down, top = hand_over(gf, feat, base, down, top)
    return (
        feat.reshape(2, 12, 16, 256),
        gf.reshape(4, 24, 32, 128),
        base.transpose(2, 0, 1),
        down.transpose(0, 2, 1),
        top.transpose(0, 2, 1),
    )


def solution(mesh):
    return jax.shard_map(
        body,
        mesh=mesh,
        in_specs=(P("tm", "row", "col", None), P(), P(), P(), P("tm", "row", "col", None)),
        out_specs=(
            P("tm", "row", "col", None),
            P("tm", "row", "col", None),
            P(None, "col", ("tm", "row")),
            P(None, "col", ("tm", "row")),
            P(None, "col", ("tm", "row")),
        ),
        check_vma=False,
    )
```

```python
import functools
import math
from types import SimpleNamespace

import jax
import jax.numpy as jnp
from jax import lax
from jax.experimental import pallas as pl
from jax.experimental.pallas import tpu as pltpu
from jax.sharding import PartitionSpec as P

F32 = jnp.float32
BF = jnp.bfloat16
ROWS = 20
TOP = 14


def dot(a, b, ca=1, cb=0):
    return lax.dot_general(a, b, (((ca,), (cb,)), ((), ())), preferred_element_type=F32)


def iota(shape, dim):
    return lax.broadcasted_iota(jnp.int32, shape, dim)


def shift_cols(value, by):
    width = value.shape[1]
    rolled = pltpu.roll(value, by % width, 1)
    gap = 0 if by > 0 else width - 1
    return jnp.where(iota(value.shape, 1) == gap, 0.0, rolled)


def pick(parts):
    out = jnp.zeros((parts[0].shape[0], 8, parts[0].shape[2]), F32)
    row = iota(out.shape, 1)
    for t, part in enumerate(parts):
        out = jnp.where(row == t, jnp.broadcast_to(part, out.shape), out)
    return out


def pack(value):
    h, _, c = value.shape
    pairs = value.reshape(h // 2, 2, 8, c)
    both = pairs[:, 0] + pltpu.roll(pairs[:, 1], 4, 1)
    return both.reshape(h // 4, 16, c).astype(BF)


def unpack_rows(groups, h):
    g, _, c = groups.shape
    pairs = groups.astype(F32).reshape(2 * g, 8, c)
    low = iota(pairs.shape, 1) < 4
    even = jnp.where(low, pairs, 0.0)
    odd = jnp.where(low, pltpu.roll(pairs, 4, 1), 0.0)
    rows = jnp.stack([even, odd], axis=1).reshape(4 * g, 8, c)
    return rows[3:h + 5]


def logistic(s):
    return 1.0 / (1.0 + jnp.exp(-s))


def weave(first, second):
    first = first.reshape(16, 8, first.shape[1])
    second = second.reshape(16, 8, second.shape[1])
    low = iota(first.shape, 1) < 4
    even = jnp.where(low, first, pltpu.roll(second, 4, 1))
    odd = jnp.where(low, pltpu.roll(first, 4, 1), second)
    return even, odd


class Halo:
    def __init__(self, comm, body, cols, land, send, recv, frames, height, back, where):
        self.comm, self.body, self.cols, self.land = comm, body, cols, land
        self.send, self.recv, self.back = send, recv, back
        self.frames, self.height, self.where = frames, height, where
        self.own = 0 if back else 2
        self.copies = []

    def start(self):
        tm, row, col = self.where
        step = -1 if self.back else 1
        h, f, own, body = self.height, self.frames, self.own, self.body
        edge = 0 if self.back else own + f - 2
        into = f if self.back else 0
        jobs = []
        for dt in (0, step):
            first, count, put = (own, f, own) if dt == 0 else (edge, 2, into)
            kind = 0 if dt == 0 else 1
            for dh in (0, 1, -1):
                src_h, n, dst_h = {0: (1, h, 1), 1: (h, 1, 0), -1: (1, 1, h + 1)}[dh]
                if dt or dh:
                    jobs.append((kind, (dt, dh, 0),
                                 body.at[pl.ds(first, count), pl.ds(src_h, n)],
                                 body.at[pl.ds(put, count), pl.ds(dst_h, n)]))
                g = h // 4
                src_g, n_g, dst_g = {0: (0, g, 1), 1: (g - 1, 1, 0), -1: (0, 1, g + 1)}[dh]
                for dw in (1, -1):
                    side = 0 if dw == 1 else 1
                    jobs.append((2, (dt, dh, dw),
                                 self.cols.at[1 - side, pl.ds(src_g, n_g)],
                                 self.land.at[side, kind, pl.ds(dst_g, n_g)]))
        jobs.sort(key=lambda job: job[0])
        if not self.comm:
            return
        for i, (kind, (dt, dh, dw), src, dst) in enumerate(jobs):
            copy = pltpu.make_async_remote_copy(
                src_ref=src, dst_ref=dst, send_sem=self.send.at[i], recv_sem=self.recv.at[i],
                device_id=((tm + dt + 8) % 8, (row + dh + 4) % 4, (col + dw + 8) % 8),
                device_id_type=pl.DeviceIdType.MESH,
            )
            copy.start()
            self.copies.append((kind, copy))

    def wait(self, kind):
        for k, copy in self.copies:
            if k == kind:
                copy.wait_recv()
        row = self.where[1]
        zero = jnp.zeros(self.body.shape[2:], BF)
        frames = range(self.own, self.own + self.frames)
        if kind == 1:
            first = self.frames if self.back else 0
            frames = range(first, first + 2)

            @pl.when(self.where[0] == (7 if self.back else 0))
            def _():
                for t in frames:
                    for r in range(self.height + 2):
                        self.body[t, r] = zero

        if kind < 2:
            @pl.when(row == 0)
            def _():
                for t in frames:
                    self.body[t, 0] = zero

            @pl.when(row == 3)
            def _():
                for t in frames:
                    self.body[t, self.height + 1] = zero

    def column(self, side):
        tm, row, col = self.where
        cur = unpack_rows(self.land[side, 0], self.height)
        far = unpack_rows(self.land[side, 1], self.height)
        shape = cur.shape
        at_t, at_h = iota(shape, 1), iota(shape, 0)
        out = col == (7 if side else 0)
        edge = tm == (7 if self.back else 0)
        if self.back:
            is_far = at_t >= self.frames
            far = pltpu.roll(far, self.frames, 1)
        else:
            is_far = at_t < 2
            far = pltpu.roll(far, 8 - (self.frames - 2), 1) if self.frames > 2 else far
            cur = pltpu.roll(cur, 2, 1)
        drop = ((at_h == 0) & (row == 0)) | ((at_h == shape[0] - 1) & (row == 3))
        drop = drop | out | (is_far & edge) | (at_t >= self.frames + 2)
        return jnp.where(drop, 0.0, jnp.where(is_far, far, cur))

    def done(self):
        for _, copy in self.copies:
            copy.wait_send()


class Reduce:
    def __init__(self, comm, s, job, r0, n, first, where):
        self.comm, self.s, self.job, self.r0, self.n = comm, s, job, r0, n
        self.first = first
        tm, row, col = where
        self.y, self.core, self.x, self.z = tm // 2, tm % 2, row, col
        self.started = []
        self.pending = {}
        self.slot = 0

    def put(self, key, src, dst, y, core, x, z):
        if not self.comm:
            return
        i = self.slot
        self.slot += 1
        copy = pltpu.make_async_remote_copy(
            src_ref=src, dst_ref=dst,
            send_sem=self.s.rs_send.at[self.job, i], recv_sem=self.s.rs_recv.at[self.job, i],
            device_id=(2 * y + core, x, z), device_id_type=pl.DeviceIdType.MESH,
        )
        copy.start()
        self.started.append(copy)
        self.pending.setdefault(key, []).append(copy)

    def arrive(self, key):
        for copy in self.pending.pop(key, []):
            copy.wait_recv()

    def a(self):
        return pl.ds(self.r0, self.first)

    def b(self):
        return pl.ds(self.r0 + self.first, self.n - self.first)

    def halves(self, part):
        r0, n = (self.r0, self.first) if part == "a" else (self.r0 + self.first, self.n - self.first)
        return pl.ds(r0, n // 2), pl.ds(r0 + n // 2, n // 2)

    def start(self, key, r0, n):
        r = pl.ds(r0, n)
        self.put("core" + key, self.s.terms.at[:, 1 - self.core, :, :, r],
                 self.s.c_land.at[:, :, :, r], self.y, 1 - self.core, self.x, self.z)

    def fold(self, key, r):
        s = self.s
        self.arrive("core" + key)

        def add(i, _):
            yy, x1, par = i // 4, (i % 4) // 2, i % 2
            s.u[yy, x1, par, r] = (
                s.terms[yy, self.core, x1, par, r].astype(F32) + s.c_land[yy, x1, par, r].astype(F32)
            ).astype(BF)
            return _

        lax.fori_loop(0, 16, add, 0, unroll=4 if self.job == 0 else 16)

    def along(self, key, part, step, unit, r, land):
        s = self.s
        if part == "a":
            to, unit = (self.y + step) % 4, (self.y + unit) % 4
            self.put(key, s.u.at[unit, :, :, r], s.da.at[land, :, :, r],
                     to, self.core, self.x, self.z)
        else:
            to, unit = (self.x + step) % 4, (self.x + unit) % 4
            self.put(key, s.u.at[:, unit // 2, unit % 2, r], s.db.at[land, :, r],
                     self.y, self.core, to, self.z)

    def send(self, part):
        self.fold(part, self.a() if part == "a" else self.b())
        p, q = self.halves(part)
        self.along("relay" + part, part, 1, 2, p, 0)
        self.along("relay" + part, part, 3, 2, q, 0)
        self.along("line" + part, part, 1, 1, q, 1)
        self.along("line" + part, part, 3, 3, p, 1)

    def relay(self, part):
        s, y, x = self.s, self.y, self.x
        self.arrive("relay" + part)
        p, q = self.halves(part)
        if part == "a":
            up, down = (y + 1) % 4, (y + 3) % 4
        else:
            up, down = (x + 1) % 4, (x + 3) % 4

        def add(i, _):
            x1, par = i // 2, i % 2
            for to, r in ((up, p), (down, q)):
                if part == "a":
                    s.g[0, x1, par, r] = (
                        s.u[to, x1, par, r].astype(F32) + s.da[0, x1, par, r].astype(F32)).astype(BF)
                else:
                    s.g[1, x1, par, r] = (
                        s.u[i, to // 2, to % 2, r].astype(F32) + s.db[0, i, r].astype(F32)).astype(BF)
            return _

        lax.fori_loop(0, 4, add, 0, unroll=4)
        for to, r in ((up, p), (down, q)):
            if part == "a":
                self.put("linea", s.g.at[0, :, :, r], s.da.at[2, :, :, r],
                         to, self.core, x, self.z)
            else:
                self.put("lineb", s.g.at[1, :, :, r], s.dc.at[:, :, r],
                         y, self.core, to, self.z)

    def planes(self):
        for part in ("a", "b"):
            self.fold(part, self.a() if part == "a" else self.b())
            for d in (2, 1, 3):
                self.along("line" + part, part, d, d, self.a() if part == "a" else self.b(), d - 1)

    def lines(self, part):
        s, y, x = self.s, self.y, self.x
        self.arrive("line" + part)

        def add(i, _):
            x1, par = i // 2, i % 2
            if part == "a":
                total = s.u[y, x1, par, self.a()].astype(F32)
                for d in range(1 if self.job == 0 else 0, 3):
                    total = total + s.da[d, x1, par, self.a()].astype(F32)
                s.va[x1, par, self.a()] = total.astype(BF)
                return _
            total = s.u[i, x // 2, x % 2, self.b()].astype(F32)
            if self.job == 0:
                total = total + s.db[1, i, self.b()].astype(F32)
                total = total + s.dc[x1, par, self.b()].astype(F32)
            else:
                for d in range(3):
                    total = total + s.db[d, i, self.b()].astype(F32)
            s.vb[i, self.b()] = total.astype(BF)
            return _

        lax.fori_loop(0, 4, add, 0, unroll=4)
        for d in (2, 1, 3):
            if part == "a":
                to = (x + d) % 4
                self.put("depth", s.va.at[to // 2, to % 2, self.a()], s.ea.at[d - 1, self.a()],
                         y, self.core, to, self.z)
            else:
                to = (y + d) % 4
                self.put("depth", s.vb.at[to, self.b()], s.eb.at[d - 1, self.b()],
                         to, self.core, x, self.z)

    def depth(self):
        s, y, x = self.s, self.y, self.x
        self.arrive("depth")
        first = s.va[x // 2, x % 2, self.a()].astype(F32)
        second = s.vb[y, self.b()].astype(F32)
        for d in range(3):
            first = first + s.ea[d, self.a()].astype(F32)
            second = second + s.eb[d, self.b()].astype(F32)
        both = jnp.concatenate([first.reshape(-1, 256), second.reshape(-1, 256)], axis=0)
        if self.job == 0:
            s.zs[...] = both.T.astype(BF).reshape(8, 32, 256)
            src, dst = s.zs, s.zr
        else:
            base = jnp.concatenate([both, jnp.zeros((64, 256), F32)], axis=0).T
            s.zs1[:, :16] = base[:128].astype(BF).reshape(8, 16, 128)
            s.zs1[:, 16:] = base[128:].astype(BF).reshape(8, 16, 128)
            src, dst = s.zs1, s.zr1
        for d in (4, 3, 5, 2, 6, 1, 7):
            to = (self.z + d) % 8
            self.put("z", src.at[to], dst.at[d - 1], y, self.core, x, to)

    def total(self):
        s = self.s
        self.arrive("z")
        src, dst = (s.zs, s.zr) if self.job == 0 else (s.zs1, s.zr1)
        total = src[self.z].astype(F32)
        if self.comm:
            for d in range(7):
                total = total + dst[d].astype(F32)
        pad = jnp.zeros((96, total.shape[1]), F32)
        return jnp.concatenate([total, pad], axis=0)

    def finish_top(self, top, down, scale):
        turned = self.total().T * scale
        top[...] = turned[:216, :32].reshape(27, 8, 32)
        for tap in range(8):
            down[tap] = turned[224 + 4 * tap:228 + 4 * tap, :32]

    def finish_base(self, out, scale):
        s = self.s
        s.fin[...] = self.total().T * scale
        parts = []
        low = iota((8, 128), 0) < 4
        for k in range(4):
            rows = s.fin[pl.ds(k, 16, stride=4), :]
            beside = pltpu.roll(rows, 112, 1)
            for j in range(2):
                first, second = rows[8 * j:8 * j + 8], beside[8 * j:8 * j + 8]
                parts.append(jnp.where(low, first, pltpu.roll(second, 4, 0)))
                parts.append(jnp.where(low, pltpu.roll(first, 4, 0), second))
        taps = jnp.concatenate(parts, axis=0).T[:16]
        for k in range(4):
            out[:, k, :] = (pltpu.roll(taps, 128 - 32 * k, 1) if k else taps)[:, :27]

    def done(self):
        for copy in self.started:
            copy.wait_send()


def scratch_list():
    dma = pltpu.SemaphoreType.DMA
    return dict(
        xe=((6, 26, 32, 128), BF),
        ge=((6, 26, 32, 128), BF),
        wf=((9, 128, 384), BF),
        wb=((384, 1152), BF),
        kd=((1024, 256), BF),
        kt=((27, 256, 256), BF),
        cot=((384, 256), BF),
        pre=((4, 768, 128), F32),
        hg=((4, 12, 2, 32, 128), F32),
        hc=((2, 2, 2, 12, 2, 16, 128), BF),
        s3=((4, 768, 384), BF),
        colx=((2, 192, 1152), BF),
        hl=((2, 192, 128), F32),
        acc=((9, 128, 384), F32),
        xf=((3, 128, 4608), BF),
        hf=((8, 128, 384), BF),
        xt=((3, 4, 14, 16, 256), BF),
        gt=((3, 4, 14, 16, 256), BF),
        acc_t=((384, 256), F32),
        grd=((384, 256), BF),
        sg=((2, 192, 128), BF),
        px=((2, 6, 16, 128), BF),
        pg=((2, 6, 16, 128), BF),
        lx=((2, 2, 8, 16, 128), BF),
        lg=((2, 2, 8, 16, 128), BF),
        pxt=((2, 3, 16, 256), BF),
        pgt=((2, 3, 16, 256), BF),
        lxt=((2, 2, 5, 16, 256), BF),
        lgt=((2, 2, 5, 16, 256), BF),
        terms=((4, 2, 2, 2, ROWS, 16, 256), BF),
        c_land=((4, 2, 2, ROWS, 16, 256), BF),
        u=((4, 2, 2, ROWS, 16, 256), BF),
        da=((3, 2, 2, ROWS, 16, 256), BF),
        db=((3, 4, ROWS, 16, 256), BF),
        va=((2, 2, ROWS, 16, 256), BF),
        vb=((4, ROWS, 16, 256), BF),
        ea=((3, ROWS, 16, 256), BF),
        eb=((3, ROWS, 16, 256), BF),
        dc=((2, 2, ROWS, 16, 256), BF),
        g=((2, 2, 2, ROWS, 16, 256), BF),
        zs=((8, 32, 256), BF),
        zr=((7, 32, 256), BF),
        zs1=((8, 32, 128), BF),
        zr1=((7, 32, 128), BF),
        fin=((128, 128), F32),
        gfs=((4, 768, 128), F32),
        feats=((384, 256), BF),
        leave=dma((5,)),
        local=dma((8,)),
        h_send=dma((4, 17)),
        h_recv=dma((4, 17)),
        rs_send=dma((2, 28)),
        rs_recv=dma((2, 28)),
    )


def base_conv(src, parts, weights, turned):
    blocks = []
    for t, h0, n in parts:
        blocks.append(jnp.concatenate(
            [src[t + a, pl.ds(h0 + b, n)].reshape(n * 32, 128) for a in range(3) for b in range(3)],
            axis=1,
        ))
    lhs = jnp.concatenate(blocks, axis=0) if len(blocks) > 1 else blocks[0]
    y = dot(lhs, weights, 1, 1 if turned else 0).reshape(-1, 32, 384)
    y = y[..., 128:256] + shift_cols(y[..., :128], 1) + shift_cols(y[..., 256:], -1)
    return y.reshape(-1, 128)


def kernel(comm, skip, scales, frames, kb, kd, kt, cot, feat, gf, out_base, out_down, out_top, *refs):
    names = list(scratch_list())
    s = SimpleNamespace(**dict(zip(names, refs)))
    if comm:
        where = (lax.axis_index("tm"), lax.axis_index("row"), lax.axis_index("col"))
    else:
        where = (jnp.int32(0), jnp.int32(0), jnp.int32(0))
    tm, row, col = where
    loads = [
        pltpu.make_async_copy(frames, s.xe.at[pl.ds(2, 4), pl.ds(1, 24)], s.local.at[0]),
        pltpu.make_async_copy(kb.at[:, 0], s.wf.at[:, :, pl.ds(0, 128)], s.local.at[1]),
        pltpu.make_async_copy(kb.at[:, 1], s.wf.at[:, :, pl.ds(128, 128)], s.local.at[2]),
        pltpu.make_async_copy(kb.at[:, 2], s.wf.at[:, :, pl.ds(256, 128)], s.local.at[3]),
        pltpu.make_async_copy(kd, s.kd, s.local.at[4]),
        pltpu.make_async_copy(kt, s.kt, s.local.at[5]),
        pltpu.make_async_copy(cot, s.cot, s.local.at[6]),
    ]
    for load in loads:
        load.start()
    halo_x = Halo(comm, s.xe, s.px, s.lx, s.h_send.at[0], s.h_recv.at[0], 4, 24, False, where)
    halo_xt = Halo(comm, s.xt.at[1], s.pxt, s.lxt, s.h_send.at[1], s.h_recv.at[1], 2, 12, False, where)
    halo_gt = Halo(comm, s.gt.at[1], s.pgt, s.lgt, s.h_send.at[2], s.h_recv.at[2], 2, 12, True, where)
    halo_g = Halo(comm, s.ge, s.pg, s.lg, s.h_send.at[3], s.h_recv.at[3], 4, 24, True, where)
    rs_top = Reduce(comm, s, 0, 0, TOP + 2, 10, where)
    rs_low = Reduce(comm, s, 1, TOP + 2, ROWS - TOP - 2, 2, where)

    if comm:
        barrier = pltpu.get_barrier_semaphore()
        near = [(a, b, c) for a in (0, 1, -1) for b in (0, 1, -1) for c in (0, 1, -1)][1:]
        far = [(2, 0, 0), (4, 0, 0), (6, 0, 0), (0, 2, 0)] + [(0, 0, d) for d in (2, 3, 4, 5, 6)]
        for dt, dh, dw in near + far:
            pl.semaphore_signal(
                barrier, inc=1,
                device_id=((tm + dt + 8) % 8, (row + dh + 4) % 4, (col + dw + 8) % 8),
                device_id_type=pl.DeviceIdType.MESH,
            )
    loads[0].wait()
    left, right = [], []
    for t in range(4):
        left.append(s.xe[2 + t, pl.ds(1, 24), pl.ds(0, 16)].astype(F32)[:, 0:1])
        right.append(s.xe[2 + t, pl.ds(1, 24), pl.ds(16, 16)].astype(F32)[:, 15:16])
    s.px[0] = pack(pick(left))
    s.px[1] = pack(pick(right))
    if comm:
        pl.semaphore_wait(barrier, len(near) + len(far))
    halo_x.start()

    for load in loads[1:4]:
        load.wait()
    for ab in range(9):
        for c in range(3):
            s.wb[c * 128:(c + 1) * 128, ab * 128:(ab + 1) * 128] = (
                s.wf[8 - ab, :, (2 - c) * 128:(3 - c) * 128])
    for load in loads[4:]:
        load.wait()

    def forward(*parts):
        value = base_conv(s.xe, parts, s.wf[...].reshape(1152, 384), False)
        at = 0
        for t, h0, n in parts:
            s.pre[t, h0 * 32:(h0 + n) * 32] = value[at:at + n * 32]
            at += n * 32

    if "fwd" not in skip:
        forward((2, 8, 8), (3, 8, 8))
        halo_x.wait(0)
        forward((2, 0, 8), (2, 16, 8))
        forward((3, 0, 8), (3, 16, 8))
        halo_x.wait(1)
        forward((0, 0, 24))
        forward((1, 0, 24))
        halo_x.wait(2)
    for side in range(2):
        column = halo_x.column(side)
        pieces = []
        for a in range(3):
            moved = pltpu.roll(column, 8 - a, 1) if a else column
            for b in range(3):
                pieces.append(moved[b:b + 24].reshape(192, 128).astype(BF))
        lhs = jnp.concatenate(pieces, axis=1)
        s.colx[side] = lhs
        c = 2 * side
        s.hl[side] = dot(lhs, s.wf[:, :, c * 128:(c + 1) * 128].reshape(1152, 128))
    for t in range(4):
        for side in range(2):
            at = pl.ds(31 * side, 24, stride=32)
            s.pre[t, at] = s.pre[t, at] + s.hl[side, pl.ds(t, 24, stride=8)]

    def act(i, _):
        t, h1 = i // 3, (i % 3) * 4
        rows = pl.ds(pl.multiple_of(h1 * 64, 256), 256)
        pre = s.pre[t, rows]
        q = logistic(pre)
        x = s.xe[2 + t, pl.ds(1 + 2 * h1, 8)].reshape(256, 128).astype(F32)
        hidden = (x + pre * q).astype(BF).astype(F32)
        s.hg[t, pl.ds(h1, 4)] = hidden.reshape(4, 2, 32, 128)
        return _

    lax.fori_loop(0, 12, act, 0)
    for t in range(4):
        for c in range(2):
            s.hc[c, t // 2, t % 2] = s.hg[t, :, :, pl.ds(c, 16, stride=2), :].astype(BF)
    taps = [(a, b, c) for a in range(2) for b in range(2) for c in range(2)]
    lhs = jnp.concatenate([s.hc[c, :, a, :, b].reshape(384, 128) for a, b, c in taps], axis=1)
    reduced = dot(lhs, s.kd[...]).astype(BF)
    red32 = reduced.astype(F32).reshape(2, 12, 16, 256)
    s.xt[1, pl.ds(2, 2), pl.ds(1, 12)] = reduced.reshape(2, 12, 16, 256)
    for side, w in ((0, 0), (1, 15)):
        s.pxt[side] = pack(pick([red32[t, :, w:w + 1] for t in range(2)]))
    halo_xt.start()

    def steep(i, _):
        t, h1 = i // 3, (i % 3) * 4
        rows = pl.ds(pl.multiple_of(h1 * 64, 256), 256)
        pre = s.pre[t, rows]
        q = logistic(pre)
        s.pre[t, rows] = q * (1.0 + pre * (1.0 - q))
        return _

    lax.fori_loop(0, 12, steep, 0)
    for f in range(6):
        for b in range(3):
            s.xf[b, :, f * 768:(f + 1) * 768] = s.xe[f, pl.ds(b, 24)].reshape(768, 128).T
    for i, (a, b, c) in enumerate(taps):
        s.hf[i] = s.hc[c, :, a, :, b].reshape(384, 128).T

    def sides(halo, ext):
        for side in range(2):
            column = halo.column(side)
            for t in range(4):
                body = ext[1, t].astype(F32)
                rolled = pltpu.roll(body, 15 if side else 1, 1)
                edge = jnp.broadcast_to(column[:, t:t + 1], body.shape)
                put = jnp.where(iota(body.shape, 1) == (15 if side else 0), edge, rolled)
                ext[2 * side, t] = put.astype(BF)

    for kind in range(3):
        halo_xt.wait(kind)
    sides(halo_xt, s.xt)

    def top_conv(ext, turned):
        for t in range(2):
            lhs = jnp.concatenate(
                [ext[c, a + t, b:b + 12].reshape(192, 256)
                 for a in range(3) for b in range(3) for c in range(3)], axis=1)
            if turned:
                rhs = jnp.concatenate([s.kt[26 - i] for i in range(27)], axis=1)
                part = dot(lhs, rhs, 1, 1)
            else:
                part = dot(lhs, s.kt[...].reshape(6912, 256))
            s.acc_t[192 * t:192 * t + 192] = part

    if "top" not in skip:
        top_conv(s.xt, False)
    pre_top = s.acc_t[...]
    q = logistic(pre_top)
    red = s.xt[1, pl.ds(2, 2), pl.ds(1, 12)].reshape(384, 256).astype(F32)
    s.feats[...] = (red + pre_top * q).astype(BF)
    leaving = [pltpu.make_async_copy(s.feats, feat, s.leave.at[4])]
    leaving[0].start()
    up = s.cot[...].astype(F32)
    slope = (up * (q * (1.0 + pre_top * (1.0 - q)))).astype(BF)
    s.grd[...] = slope
    slope32 = slope.astype(F32).reshape(2, 12, 16, 256)
    s.gt[1, pl.ds(0, 2), pl.ds(1, 12)] = slope.reshape(2, 12, 16, 256)
    for side, w in ((0, 0), (1, 15)):
        s.pgt[side] = pack(pick([slope32[t, :, w:w + 1] for t in range(2)]))
    halo_gt.start()

    def top_taps(abs_):
        lhs = jnp.concatenate(
            [s.xt[c, pl.ds(ab // 3, 2), pl.ds(ab % 3, 12)].reshape(384, 256)
             for ab in abs_ for c in range(3)], axis=1)
        return dot(lhs, s.grd[...], 0, 0).reshape(-1, 32, 8, 256)

    def top_store(r, first, second):
        both = jnp.concatenate([first, second], axis=1)
        s.terms[:, :, :, :, r] = both.astype(BF).reshape(4, 2, 2, 2, 16, 256)

    def top_six(i, _):
        group = top_taps([2 * i, 2 * i + 1])
        for k in range(3):
            top_store(3 * i + k, group[2 * k], group[2 * k + 1])
        return _

    if "tgrad" not in skip:
        lax.fori_loop(0, 4, top_six, 0)
    rs_top.start("a", 0, 10)
    group = top_taps([8])
    top_store(12, group[0], group[1])
    top_store(13, group[2], jnp.zeros((32, 8, 256), F32))
    rs_top.start("b", 10, TOP - 10)

    for kind in range(3):
        halo_gt.wait(kind)
    sides(halo_gt, s.gt)
    if "top" not in skip:
        top_conv(s.gt, True)
    rs_top.send("a")
    grad_red = (s.cot[...].astype(F32) + s.acc_t[...]).astype(BF)
    s.grd[...] = grad_red

    def store_low(r, lanes, group):
        first, second = weave(group[0], group[1]), weave(group[2], group[3])
        for par in range(2):
            both = jnp.concatenate([first[par], second[par]], axis=1).astype(BF)
            s.terms[:, :, :, par, r, :, lanes] = both.reshape(4, 2, 2, 16, both.shape[2])

    terms = dot(s.hf[...].reshape(1024, 384), s.grd[...]).reshape(8, 128, 256)
    for g in range(2):
        store_low(TOP + g, slice(0, 256), [terms[4 * g + i] for i in range(4)])
    rs_top.start("b", TOP, 2)

    spread = dot(grad_red, s.kd[...], 1, 1)
    for i, (a, b, c) in enumerate(taps):
        part = spread[:, i * 128:(i + 1) * 128].reshape(2, 12, 16, 128)
        for t in range(2):
            s.hg[2 * t + a, :, b, pl.ds(c, 16, stride=2), :] = part[t]

    low, high = [], []
    for t in range(4):
        gh = s.hg[t].reshape(24, 32, 128)
        slope = (gh * s.pre[t].reshape(24, 32, 128)).astype(BF)
        s.ge[t, pl.ds(1, 24)] = slope
        slope32 = slope.astype(F32)
        low.append(slope32[:, 0:1])
        high.append(slope32[:, 31:32])
        s.s3[t, :, 128:256] = slope.reshape(768, 128)
        s.s3[t, :, :128] = shift_cols(slope32, -1).astype(BF).reshape(768, 128)
        s.s3[t, :, 256:] = shift_cols(slope32, 1).astype(BF).reshape(768, 128)
    for side, parts in enumerate((low, high)):
        edge = pick(parts)
        s.pg[side] = pack(edge)
        s.sg[side] = edge.reshape(192, 128).astype(BF)
    halo_g.start()
    rs_top.send("b")

    def base_taps(a):
        lhs = s.xf[:, :, a * 768:a * 768 + 3072].reshape(384, 3072)
        total = dot(lhs, s.s3[...].reshape(3072, 384))
        s.acc[3 * a:3 * a + 3] = total.reshape(3, 128, 384)

    if "bgrad" not in skip:
        base_taps(0)
    rs_top.relay("a")
    if "bgrad" not in skip:
        base_taps(1)
        base_taps(2)
    rs_top.relay("b")
    for side in range(2):
        extra = dot(s.colx[side], s.sg[side], 0, 0)
        lanes = slice(256 * side, 256 * side + 128)
        s.acc[:, :, lanes] = s.acc[:, :, lanes] + extra.reshape(9, 128, 128)
    for g in range(7):
        group = []
        for tap in range(4 * g, 4 * g + 4):
            if tap < 27:
                c = tap % 3
                group.append(s.acc[tap // 3, :, c * 128:(c + 1) * 128])
            else:
                group.append(jnp.zeros((128, 128), F32))
        store_low(TOP + 2 + g // 2, slice(128 * (g % 2), 128 * (g % 2) + 128), group)
    s.terms[:, :, :, :, ROWS - 1, :, 128:] = jnp.zeros((4, 2, 2, 2, 16, 128), BF)
    rs_low.start("a", TOP + 2, ROWS - TOP - 2)
    rs_top.lines("a")

    for kind in range(3):
        halo_g.wait(kind)
    for side in range(2):
        column = halo_g.column(side)
        pieces = []
        for a in range(3):
            moved = pltpu.roll(column, 8 - a, 1) if a else column
            for b in range(3):
                pieces.append(moved[b:b + 24].reshape(192, 128).astype(BF))
        lhs = jnp.concatenate(pieces, axis=1)
        c = 2 * side
        s.hl[side] = dot(lhs, s.wb[c * 128:(c + 1) * 128, :], 1, 1)

    def backward(t):
        value = base_conv(s.ge, [(t, 0, 24)], s.wb[...], True)
        s.gfs[t] = s.hg[t].reshape(768, 128) + value
        for side in range(2):
            at = pl.ds(31 * side, 24, stride=32)
            s.gfs[t, at] = s.gfs[t, at] + s.hl[side, pl.ds(t, 24, stride=8)]
        copy = pltpu.make_async_copy(s.gfs.at[t], gf.at[t], s.leave.at[t])
        copy.start()
        leaving.append(copy)

    backward(0)
    rs_low.planes()
    rs_top.lines("b")
    backward(1)
    backward(2)
    rs_low.lines("a")
    rs_low.lines("b")
    rs_top.depth()
    backward(3)
    rs_low.depth()
    rs_top.finish_top(out_top, out_down, scales[1])
    rs_low.finish_base(out_base, scales[0])
    for copy in leaving:
        copy.wait()
    for user in (halo_x, halo_xt, halo_gt, halo_g, rs_top, rs_low):
        user.done()


def call(comm, skip, scales, *args):
    scratch = [pltpu.VMEM(*v) if isinstance(v, tuple) else v for v in scratch_list().values()]
    vmem = pl.BlockSpec(memory_space=pltpu.VMEM)
    params = dict(collective_id=0, has_side_effects=True) if comm else {}
    return pl.pallas_call(
        functools.partial(kernel, comm, skip, scales),
        out_shape=(
            jax.ShapeDtypeStruct((384, 256), BF),
            jax.ShapeDtypeStruct((4, 768, 128), F32),
            jax.ShapeDtypeStruct((16, 4, 27), F32),
            jax.ShapeDtypeStruct((8, 4, 32), F32),
            jax.ShapeDtypeStruct((27, 8, 32), F32),
        ),
        in_specs=[pl.BlockSpec(memory_space=pl.ANY)] * 5,
        out_specs=(pl.BlockSpec(memory_space=pl.ANY),) * 2 + (vmem,) * 3,
        scratch_shapes=scratch,
        compiler_params=pltpu.CompilerParams(vmem_limit_bytes=60 * 1024 * 1024, **params),
        cost_estimate=pl.CostEstimate(flops=13 * 10**9, bytes_accessed=10**7, transcendentals=10**6),
    )(*args)


def hand_over_kernel(*refs):
    n = (len(refs) - 2) // 3
    come, go = refs[-2:]
    pieces = []
    for src, dst, mid in zip(refs[:n], refs[n:2 * n], refs[2 * n:3 * n]):
        if src.shape[0] == 4:
            pieces += [(src.at[t], mid.at[t], dst.at[t]) for t in range(4)]
        else:
            pieces.append((src, mid, dst))
    inward = [pltpu.make_async_copy(a, b, come.at[i]) for i, (a, b, c) in enumerate(pieces)]
    outward = [pltpu.make_async_copy(b, c, go.at[i]) for i, (a, b, c) in enumerate(pieces)]
    for copy in inward:
        copy.start()
    for copy, after in zip(inward, outward):
        copy.wait()
        after.start()
    for copy in outward:
        copy.wait()


def hand_over(*arrays):
    n = len(arrays) + 3
    return pl.pallas_call(
        hand_over_kernel,
        out_shape=tuple(jax.ShapeDtypeStruct(a.shape, a.dtype) for a in arrays),
        in_specs=[pl.BlockSpec(memory_space=pl.ANY)] * len(arrays),
        out_specs=tuple(pl.BlockSpec(memory_space=pl.ANY) for _ in arrays),
        scratch_shapes=[pltpu.VMEM(a.shape, a.dtype) for a in arrays]
        + [pltpu.SemaphoreType.DMA((n,)), pltpu.SemaphoreType.DMA((n,))],
    )(*arrays)


def body(frames_in, kernel_base, kernel_down, kernel_top, cotangent, comm=True, skip=()):
    devices = 1
    if comm:
        devices = lax.axis_size("tm") * lax.axis_size("row") * lax.axis_size("col")
    scales = (1.0 / math.sqrt(devices * 3072), 1.0 / math.sqrt(devices * 384))
    feat, gf, base, down, top = call(
        comm, skip, scales,
        frames_in,
        kernel_base.reshape(9, 3, 128, 128),
        kernel_down.reshape(1024, 256),
        kernel_top.reshape(27, 256, 256),
        cotangent.reshape(384, 256),
    )
    gf, feat, base, down, top = hand_over(gf, feat, base, down, top)
    return (
        feat.reshape(2, 12, 16, 256),
        gf.reshape(4, 24, 32, 128),
        base.transpose(2, 0, 1),
        down.transpose(0, 2, 1),
        top.transpose(0, 2, 1),
    )


def solution(mesh):
    return jax.shard_map(
        body,
        mesh=mesh,
        in_specs=(P("tm", "row", "col", None), P(), P(), P(), P("tm", "row", "col", None)),
        out_specs=(
            P("tm", "row", "col", None),
            P("tm", "row", "col", None),
            P(None, "col", ("tm", "row")),
            P(None, "col", ("tm", "row")),
            P(None, "col", ("tm", "row")),
        ),
        check_vma=False,
    )
```

```python
import functools
import math
from types import SimpleNamespace

import jax
import jax.numpy as jnp
from jax import lax
from jax.experimental import pallas as pl
from jax.experimental.pallas import tpu as pltpu
from jax.sharding import PartitionSpec as P

F32 = jnp.float32
BF = jnp.bfloat16
ROWS = 20
TOP = 14


def dot(a, b, ca=1, cb=0):
    return lax.dot_general(a, b, (((ca,), (cb,)), ((), ())), preferred_element_type=F32)


def iota(shape, dim):
    return lax.broadcasted_iota(jnp.int32, shape, dim)


def shift_cols(value, by):
    width = value.shape[1]
    rolled = pltpu.roll(value, by % width, 1)
    gap = 0 if by > 0 else width - 1
    return jnp.where(iota(value.shape, 1) == gap, 0.0, rolled)


def pick(parts):
    out = jnp.zeros((parts[0].shape[0], 8, parts[0].shape[2]), F32)
    row = iota(out.shape, 1)
    for t, part in enumerate(parts):
        out = jnp.where(row == t, jnp.broadcast_to(part, out.shape), out)
    return out


def pack(value):
    h, _, c = value.shape
    pairs = value.reshape(h // 2, 2, 8, c)
    both = pairs[:, 0] + pltpu.roll(pairs[:, 1], 4, 1)
    return both.reshape(h // 4, 16, c).astype(BF)


def unpack_rows(groups, h):
    g, _, c = groups.shape
    pairs = groups.astype(F32).reshape(2 * g, 8, c)
    low = iota(pairs.shape, 1) < 4
    even = jnp.where(low, pairs, 0.0)
    odd = jnp.where(low, pltpu.roll(pairs, 4, 1), 0.0)
    rows = jnp.stack([even, odd], axis=1).reshape(4 * g, 8, c)
    return rows[3:h + 5]


def logistic(s):
    return 1.0 / (1.0 + jnp.exp(-s))


def weave(first, second):
    first = first.reshape(16, 8, first.shape[1])
    second = second.reshape(16, 8, second.shape[1])
    low = iota(first.shape, 1) < 4
    even = jnp.where(low, first, pltpu.roll(second, 4, 1))
    odd = jnp.where(low, pltpu.roll(first, 4, 1), second)
    return even, odd


class Halo:
    def __init__(self, comm, body, cols, land, send, recv, frames, height, back, where):
        self.comm, self.body, self.cols, self.land = comm, body, cols, land
        self.send, self.recv, self.back = send, recv, back
        self.frames, self.height, self.where = frames, height, where
        self.own = 0 if back else 2
        self.copies = []

    def start(self):
        tm, row, col = self.where
        step = -1 if self.back else 1
        h, f, own, body = self.height, self.frames, self.own, self.body
        edge = 0 if self.back else own + f - 2
        into = f if self.back else 0
        jobs = []
        for dt in (0, step):
            first, count, put = (own, f, own) if dt == 0 else (edge, 2, into)
            kind = 0 if dt == 0 else 1
            for dh in (0, 1, -1):
                src_h, n, dst_h = {0: (1, h, 1), 1: (h, 1, 0), -1: (1, 1, h + 1)}[dh]
                if dt or dh:
                    jobs.append((kind, (dt, dh, 0),
                                 body.at[pl.ds(first, count), pl.ds(src_h, n)],
                                 body.at[pl.ds(put, count), pl.ds(dst_h, n)]))
                g = h // 4
                src_g, n_g, dst_g = {0: (0, g, 1), 1: (g - 1, 1, 0), -1: (0, 1, g + 1)}[dh]
                for dw in (1, -1):
                    side = 0 if dw == 1 else 1
                    jobs.append((2, (dt, dh, dw),
                                 self.cols.at[1 - side, pl.ds(src_g, n_g)],
                                 self.land.at[side, kind, pl.ds(dst_g, n_g)]))
        jobs.sort(key=lambda job: job[0])
        if not self.comm:
            return
        for i, (kind, (dt, dh, dw), src, dst) in enumerate(jobs):
            copy = pltpu.make_async_remote_copy(
                src_ref=src, dst_ref=dst, send_sem=self.send.at[i], recv_sem=self.recv.at[i],
                device_id=((tm + dt + 8) % 8, (row + dh + 4) % 4, (col + dw + 8) % 8),
                device_id_type=pl.DeviceIdType.MESH,
            )
            copy.start()
            self.copies.append((kind, copy))

    def wait(self, kind):
        for k, copy in self.copies:
            if k == kind:
                copy.wait_recv()
        row = self.where[1]
        zero = jnp.zeros(self.body.shape[2:], BF)
        frames = range(self.own, self.own + self.frames)
        if kind == 1:
            first = self.frames if self.back else 0
            frames = range(first, first + 2)

            @pl.when(self.where[0] == (7 if self.back else 0))
            def _():
                for t in frames:
                    for r in range(self.height + 2):
                        self.body[t, r] = zero

        if kind < 2:
            @pl.when(row == 0)
            def _():
                for t in frames:
                    self.body[t, 0] = zero

            @pl.when(row == 3)
            def _():
                for t in frames:
                    self.body[t, self.height + 1] = zero

    def column(self, side):
        tm, row, col = self.where
        cur = unpack_rows(self.land[side, 0], self.height)
        far = unpack_rows(self.land[side, 1], self.height)
        shape = cur.shape
        at_t, at_h = iota(shape, 1), iota(shape, 0)
        out = col == (7 if side else 0)
        edge = tm == (7 if self.back else 0)
        if self.back:
            is_far = at_t >= self.frames
            far = pltpu.roll(far, self.frames, 1)
        else:
            is_far = at_t < 2
            far = pltpu.roll(far, 8 - (self.frames - 2), 1) if self.frames > 2 else far
            cur = pltpu.roll(cur, 2, 1)
        drop = ((at_h == 0) & (row == 0)) | ((at_h == shape[0] - 1) & (row == 3))
        drop = drop | out | (is_far & edge) | (at_t >= self.frames + 2)
        return jnp.where(drop, 0.0, jnp.where(is_far, far, cur))

    def done(self):
        for _, copy in self.copies:
            copy.wait_send()


class Reduce:
    def __init__(self, comm, s, job, r0, n, first, where):
        self.comm, self.s, self.job, self.r0, self.n = comm, s, job, r0, n
        self.first = first
        tm, row, col = where
        self.y, self.core, self.x, self.z = tm // 2, tm % 2, row, col
        self.started = []
        self.pending = {}
        self.slot = 0

    def put(self, key, src, dst, y, core, x, z):
        if not self.comm:
            return
        i = self.slot
        self.slot += 1
        copy = pltpu.make_async_remote_copy(
            src_ref=src, dst_ref=dst,
            send_sem=self.s.rs_send.at[self.job, i], recv_sem=self.s.rs_recv.at[self.job, i],
            device_id=(2 * y + core, x, z), device_id_type=pl.DeviceIdType.MESH,
        )
        copy.start()
        self.started.append(copy)
        self.pending.setdefault(key, []).append(copy)

    def arrive(self, key):
        for copy in self.pending.pop(key, []):
            copy.wait_recv()

    def a(self):
        return pl.ds(self.r0, self.first)

    def b(self):
        return pl.ds(self.r0 + self.first, self.n - self.first)

    def halves(self, part):
        r0, n = (self.r0, self.first) if part == "a" else (self.r0 + self.first, self.n - self.first)
        return pl.ds(r0, n // 2), pl.ds(r0 + n // 2, n // 2)

    def start(self, key, r0, n):
        r = pl.ds(r0, n)
        self.put("core" + key, self.s.terms.at[:, 1 - self.core, :, :, r],
                 self.s.c_land.at[:, :, :, r], self.y, 1 - self.core, self.x, self.z)

    def fold(self, key, r):
        s = self.s
        self.arrive("core" + key)

        def add(i, _):
            yy, x1, par = i // 4, (i % 4) // 2, i % 2
            s.u[yy, x1, par, r] = (
                s.terms[yy, self.core, x1, par, r].astype(F32) + s.c_land[yy, x1, par, r].astype(F32)
            ).astype(BF)
            return _

        lax.fori_loop(0, 16, add, 0, unroll=4 if self.job == 0 else 16)

    def along(self, key, part, step, unit, r, land):
        s = self.s
        if part == "a":
            to, unit = (self.y + step) % 4, (self.y + unit) % 4
            self.put(key, s.u.at[unit, :, :, r], s.da.at[land, :, :, r],
                     to, self.core, self.x, self.z)
        else:
            to, unit = (self.x + step) % 4, (self.x + unit) % 4
            self.put(key, s.u.at[:, unit // 2, unit % 2, r], s.db.at[land, :, r],
                     self.y, self.core, to, self.z)

    def send(self, part):
        self.fold(part, self.a() if part == "a" else self.b())
        p, q = self.halves(part)
        self.along("relay" + part, part, 1, 2, p, 0)
        self.along("relay" + part, part, 3, 2, q, 0)
        self.along("line" + part, part, 1, 1, q, 1)
        self.along("line" + part, part, 3, 3, p, 1)

    def relay(self, part):
        s, y, x = self.s, self.y, self.x
        self.arrive("relay" + part)
        p, q = self.halves(part)
        if part == "a":
            up, down = (y + 1) % 4, (y + 3) % 4
        else:
            up, down = (x + 1) % 4, (x + 3) % 4

        def add(i, _):
            x1, par = i // 2, i % 2
            for to, r in ((up, p), (down, q)):
                if part == "a":
                    s.g[0, x1, par, r] = (
                        s.u[to, x1, par, r].astype(F32) + s.da[0, x1, par, r].astype(F32)).astype(BF)
                else:
                    s.g[1, x1, par, r] = (
                        s.u[i, to // 2, to % 2, r].astype(F32) + s.db[0, i, r].astype(F32)).astype(BF)
            return _

        lax.fori_loop(0, 4, add, 0, unroll=4)
        for to, r in ((up, p), (down, q)):
            if part == "a":
                self.put("linea", s.g.at[0, :, :, r], s.da.at[2, :, :, r],
                         to, self.core, x, self.z)
            else:
                self.put("lineb", s.g.at[1, :, :, r], s.dc.at[:, :, r],
                         y, self.core, to, self.z)

    def planes(self, part):
        groups = self.a() if part == "a" else self.b()
        self.fold(part, groups)
        for d in (2, 1, 3):
            self.along("line" + part, part, d, d, groups, d - 1)

    def lines(self, part):
        s, y, x = self.s, self.y, self.x
        self.arrive("line" + part)

        def add(i, _):
            x1, par = i // 2, i % 2
            if part == "a":
                total = s.u[y, x1, par, self.a()].astype(F32)
                for d in range(1 if self.job == 0 else 0, 3):
                    total = total + s.da[d, x1, par, self.a()].astype(F32)
                s.va[x1, par, self.a()] = total.astype(BF)
                return _
            total = s.u[i, x // 2, x % 2, self.b()].astype(F32)
            if self.job == 0:
                total = total + s.db[1, i, self.b()].astype(F32)
                total = total + s.dc[x1, par, self.b()].astype(F32)
            else:
                for d in range(3):
                    total = total + s.db[d, i, self.b()].astype(F32)
            s.vb[i, self.b()] = total.astype(BF)
            return _

        lax.fori_loop(0, 4, add, 0, unroll=4)
        for d in (2, 1, 3):
            if part == "a":
                to = (x + d) % 4
                self.put("depth", s.va.at[to // 2, to % 2, self.a()], s.ea.at[d - 1, self.a()],
                         y, self.core, to, self.z)
            else:
                to = (y + d) % 4
                self.put("depth", s.vb.at[to, self.b()], s.eb.at[d - 1, self.b()],
                         to, self.core, x, self.z)

    def depth(self):
        s, y, x = self.s, self.y, self.x
        self.arrive("depth")
        first = s.va[x // 2, x % 2, self.a()].astype(F32)
        second = s.vb[y, self.b()].astype(F32)
        for d in range(3):
            first = first + s.ea[d, self.a()].astype(F32)
            second = second + s.eb[d, self.b()].astype(F32)
        both = jnp.concatenate([first.reshape(-1, 256), second.reshape(-1, 256)], axis=0)
        if self.job == 0:
            s.zs[...] = both.T.astype(BF).reshape(8, 32, 256)
            src, dst = s.zs, s.zr
        else:
            base = jnp.concatenate([both, jnp.zeros((64, 256), F32)], axis=0).T
            s.zs1[:, :16] = base[:128].astype(BF).reshape(8, 16, 128)
            s.zs1[:, 16:] = base[128:].astype(BF).reshape(8, 16, 128)
            src, dst = s.zs1, s.zr1
        for d in (4, 3, 5, 2, 6, 1, 7):
            to = (self.z + d) % 8
            self.put("z", src.at[to], dst.at[d - 1], y, self.core, x, to)

    def total(self):
        s = self.s
        self.arrive("z")
        src, dst = (s.zs, s.zr) if self.job == 0 else (s.zs1, s.zr1)
        total = src[self.z].astype(F32)
        if self.comm:
            for d in range(7):
                total = total + dst[d].astype(F32)
        pad = jnp.zeros((96, total.shape[1]), F32)
        return jnp.concatenate([total, pad], axis=0)

    def finish_top(self, top, down, scale):
        turned = self.total().T * scale
        top[...] = turned[:216, :32].reshape(27, 8, 32)
        for tap in range(8):
            down[tap] = turned[224 + 4 * tap:228 + 4 * tap, :32]

    def finish_base(self, out, scale):
        s = self.s
        s.fin[...] = self.total().T * scale
        parts = []
        low = iota((8, 128), 0) < 4
        for k in range(4):
            rows = s.fin[pl.ds(k, 16, stride=4), :]
            beside = pltpu.roll(rows, 112, 1)
            for j in range(2):
                first, second = rows[8 * j:8 * j + 8], beside[8 * j:8 * j + 8]
                parts.append(jnp.where(low, first, pltpu.roll(second, 4, 0)))
                parts.append(jnp.where(low, pltpu.roll(first, 4, 0), second))
        taps = jnp.concatenate(parts, axis=0).T[:16]
        for k in range(4):
            out[:, k, :] = (pltpu.roll(taps, 128 - 32 * k, 1) if k else taps)[:, :27]

    def done(self):
        for copy in self.started:
            copy.wait_send()


def scratch_list():
    dma = pltpu.SemaphoreType.DMA
    return dict(
        xe=((6, 26, 32, 128), BF),
        ge=((6, 26, 32, 128), BF),
        wf=((9, 128, 384), BF),
        wb=((384, 1152), BF),
        kd=((1024, 256), BF),
        kt=((27, 256, 256), BF),
        cot=((384, 256), BF),
        pre=((4, 768, 128), F32),
        hg=((4, 12, 2, 32, 128), F32),
        hc=((2, 2, 2, 12, 2, 16, 128), BF),
        s3=((4, 768, 384), BF),
        colx=((2, 192, 1152), BF),
        hl=((2, 192, 128), F32),
        acc=((9, 128, 384), F32),
        xf=((3, 128, 4608), BF),
        hf=((8, 128, 384), BF),
        xt=((3, 4, 14, 16, 256), BF),
        gt=((3, 4, 14, 16, 256), BF),
        acc_t=((384, 256), F32),
        grd=((384, 256), BF),
        sg=((2, 192, 128), BF),
        px=((2, 6, 16, 128), BF),
        pg=((2, 6, 16, 128), BF),
        lx=((2, 2, 8, 16, 128), BF),
        lg=((2, 2, 8, 16, 128), BF),
        pxt=((2, 3, 16, 256), BF),
        pgt=((2, 3, 16, 256), BF),
        lxt=((2, 2, 5, 16, 256), BF),
        lgt=((2, 2, 5, 16, 256), BF),
        terms=((4, 2, 2, 2, ROWS, 16, 256), BF),
        c_land=((4, 2, 2, ROWS, 16, 256), BF),
        u=((4, 2, 2, ROWS, 16, 256), BF),
        da=((3, 2, 2, ROWS, 16, 256), BF),
        db=((3, 4, ROWS, 16, 256), BF),
        va=((2, 2, ROWS, 16, 256), BF),
        vb=((4, ROWS, 16, 256), BF),
        ea=((3, ROWS, 16, 256), BF),
        eb=((3, ROWS, 16, 256), BF),
        dc=((2, 2, ROWS, 16, 256), BF),
        g=((2, 2, 2, ROWS, 16, 256), BF),
        zs=((8, 32, 256), BF),
        zr=((7, 32, 256), BF),
        zs1=((8, 32, 128), BF),
        zr1=((7, 32, 128), BF),
        fin=((128, 128), F32),
        gfs=((4, 768, 128), F32),
        feats=((384, 256), BF),
        leave=dma((5,)),
        local=dma((8,)),
        h_send=dma((4, 17)),
        h_recv=dma((4, 17)),
        rs_send=dma((2, 28)),
        rs_recv=dma((2, 28)),
    )


def base_conv(src, parts, weights, turned):
    blocks = []
    for t, h0, n in parts:
        blocks.append(jnp.concatenate(
            [src[t + a, pl.ds(h0 + b, n)].reshape(n * 32, 128) for a in range(3) for b in range(3)],
            axis=1,
        ))
    lhs = jnp.concatenate(blocks, axis=0) if len(blocks) > 1 else blocks[0]
    y = dot(lhs, weights, 1, 1 if turned else 0).reshape(-1, 32, 384)
    y = y[..., 128:256] + shift_cols(y[..., :128], 1) + shift_cols(y[..., 256:], -1)
    return y.reshape(-1, 128)


def kernel(comm, skip, scales, frames, kb, kd, kt, cot, feat, gf, out_base, out_down, out_top, *refs):
    names = list(scratch_list())
    s = SimpleNamespace(**dict(zip(names, refs)))
    if comm:
        where = (lax.axis_index("tm"), lax.axis_index("row"), lax.axis_index("col"))
    else:
        where = (jnp.int32(0), jnp.int32(0), jnp.int32(0))
    tm, row, col = where
    loads = [
        pltpu.make_async_copy(frames, s.xe.at[pl.ds(2, 4), pl.ds(1, 24)], s.local.at[0]),
        pltpu.make_async_copy(kb.at[:, 0], s.wf.at[:, :, pl.ds(0, 128)], s.local.at[1]),
        pltpu.make_async_copy(kb.at[:, 1], s.wf.at[:, :, pl.ds(128, 128)], s.local.at[2]),
        pltpu.make_async_copy(kb.at[:, 2], s.wf.at[:, :, pl.ds(256, 128)], s.local.at[3]),
        pltpu.make_async_copy(kd, s.kd, s.local.at[4]),
        pltpu.make_async_copy(kt, s.kt, s.local.at[5]),
        pltpu.make_async_copy(cot, s.cot, s.local.at[6]),
    ]
    for load in loads:
        load.start()
    halo_x = Halo(comm, s.xe, s.px, s.lx, s.h_send.at[0], s.h_recv.at[0], 4, 24, False, where)
    halo_xt = Halo(comm, s.xt.at[1], s.pxt, s.lxt, s.h_send.at[1], s.h_recv.at[1], 2, 12, False, where)
    halo_gt = Halo(comm, s.gt.at[1], s.pgt, s.lgt, s.h_send.at[2], s.h_recv.at[2], 2, 12, True, where)
    halo_g = Halo(comm, s.ge, s.pg, s.lg, s.h_send.at[3], s.h_recv.at[3], 4, 24, True, where)
    rs_top = Reduce(comm, s, 0, 0, TOP + 2, 10, where)
    rs_low = Reduce(comm, s, 1, TOP + 2, ROWS - TOP - 2, 2, where)

    if comm:
        barrier = pltpu.get_barrier_semaphore()
        near = [(a, b, c) for a in (0, 1, -1) for b in (0, 1, -1) for c in (0, 1, -1)][1:]
        far = [(2, 0, 0), (4, 0, 0), (6, 0, 0), (0, 2, 0)] + [(0, 0, d) for d in (2, 3, 4, 5, 6)]
        for dt, dh, dw in near + far:
            pl.semaphore_signal(
                barrier, inc=1,
                device_id=((tm + dt + 8) % 8, (row + dh + 4) % 4, (col + dw + 8) % 8),
                device_id_type=pl.DeviceIdType.MESH,
            )
    loads[0].wait()
    left, right = [], []
    for t in range(4):
        left.append(s.xe[2 + t, pl.ds(1, 24), pl.ds(0, 16)].astype(F32)[:, 0:1])
        right.append(s.xe[2 + t, pl.ds(1, 24), pl.ds(16, 16)].astype(F32)[:, 15:16])
    s.px[0] = pack(pick(left))
    s.px[1] = pack(pick(right))
    if comm:
        pl.semaphore_wait(barrier, len(near) + len(far))
    halo_x.start()

    for load in loads[1:4]:
        load.wait()
    for ab in range(9):
        for c in range(3):
            s.wb[c * 128:(c + 1) * 128, ab * 128:(ab + 1) * 128] = (
                s.wf[8 - ab, :, (2 - c) * 128:(3 - c) * 128])
    for load in loads[4:]:
        load.wait()

    def forward(*parts):
        value = base_conv(s.xe, parts, s.wf[...].reshape(1152, 384), False)
        at = 0
        for t, h0, n in parts:
            s.pre[t, h0 * 32:(h0 + n) * 32] = value[at:at + n * 32]
            at += n * 32

    if "fwd" not in skip:
        forward((2, 8, 8), (3, 8, 8))
        halo_x.wait(0)
        forward((2, 0, 8), (2, 16, 8))
        forward((3, 0, 8), (3, 16, 8))
        halo_x.wait(1)
        forward((0, 0, 24))
        forward((1, 0, 24))
        halo_x.wait(2)
    for side in range(2):
        column = halo_x.column(side)
        pieces = []
        for a in range(3):
            moved = pltpu.roll(column, 8 - a, 1) if a else column
            for b in range(3):
                pieces.append(moved[b:b + 24].reshape(192, 128).astype(BF))
        lhs = jnp.concatenate(pieces, axis=1)
        s.colx[side] = lhs
        c = 2 * side
        s.hl[side] = dot(lhs, s.wf[:, :, c * 128:(c + 1) * 128].reshape(1152, 128))
    for t in range(4):
        for side in range(2):
            at = pl.ds(31 * side, 24, stride=32)
            s.pre[t, at] = s.pre[t, at] + s.hl[side, pl.ds(t, 24, stride=8)]

    def act(i, _):
        t, h1 = i // 3, (i % 3) * 4
        rows = pl.ds(pl.multiple_of(h1 * 64, 256), 256)
        pre = s.pre[t, rows]
        q = logistic(pre)
        x = s.xe[2 + t, pl.ds(1 + 2 * h1, 8)].reshape(256, 128).astype(F32)
        hidden = (x + pre * q).astype(BF).astype(F32)
        s.hg[t, pl.ds(h1, 4)] = hidden.reshape(4, 2, 32, 128)
        return _

    lax.fori_loop(0, 12, act, 0)
    for t in range(4):
        for c in range(2):
            s.hc[c, t // 2, t % 2] = s.hg[t, :, :, pl.ds(c, 16, stride=2), :].astype(BF)
    taps = [(a, b, c) for a in range(2) for b in range(2) for c in range(2)]
    lhs = jnp.concatenate([s.hc[c, :, a, :, b].reshape(384, 128) for a, b, c in taps], axis=1)
    reduced = dot(lhs, s.kd[...]).astype(BF)
    red32 = reduced.astype(F32).reshape(2, 12, 16, 256)
    s.xt[1, pl.ds(2, 2), pl.ds(1, 12)] = reduced.reshape(2, 12, 16, 256)
    for side, w in ((0, 0), (1, 15)):
        s.pxt[side] = pack(pick([red32[t, :, w:w + 1] for t in range(2)]))
    halo_xt.start()

    def steep(i, _):
        t, h1 = i // 3, (i % 3) * 4
        rows = pl.ds(pl.multiple_of(h1 * 64, 256), 256)
        pre = s.pre[t, rows]
        q = logistic(pre)
        s.pre[t, rows] = q * (1.0 + pre * (1.0 - q))
        return _

    lax.fori_loop(0, 12, steep, 0)
    for f in range(6):
        for b in range(3):
            s.xf[b, :, f * 768:(f + 1) * 768] = s.xe[f, pl.ds(b, 24)].reshape(768, 128).T
    for i, (a, b, c) in enumerate(taps):
        s.hf[i] = s.hc[c, :, a, :, b].reshape(384, 128).T

    def sides(halo, ext):
        for side in range(2):
            column = halo.column(side)
            for t in range(4):
                body = ext[1, t].astype(F32)
                rolled = pltpu.roll(body, 15 if side else 1, 1)
                edge = jnp.broadcast_to(column[:, t:t + 1], body.shape)
                put = jnp.where(iota(body.shape, 1) == (15 if side else 0), edge, rolled)
                ext[2 * side, t] = put.astype(BF)

    for kind in range(3):
        halo_xt.wait(kind)
    sides(halo_xt, s.xt)

    def top_conv(ext, turned):
        for t in range(2):
            lhs = jnp.concatenate(
                [ext[c, a + t, b:b + 12].reshape(192, 256)
                 for a in range(3) for b in range(3) for c in range(3)], axis=1)
            if turned:
                rhs = jnp.concatenate([s.kt[26 - i] for i in range(27)], axis=1)
                part = dot(lhs, rhs, 1, 1)
            else:
                part = dot(lhs, s.kt[...].reshape(6912, 256))
            s.acc_t[192 * t:192 * t + 192] = part

    if "top" not in skip:
        top_conv(s.xt, False)
    pre_top = s.acc_t[...]
    q = logistic(pre_top)
    red = s.xt[1, pl.ds(2, 2), pl.ds(1, 12)].reshape(384, 256).astype(F32)
    s.feats[...] = (red + pre_top * q).astype(BF)
    leaving = [pltpu.make_async_copy(s.feats, feat, s.leave.at[4])]
    leaving[0].start()
    up = s.cot[...].astype(F32)
    slope = (up * (q * (1.0 + pre_top * (1.0 - q)))).astype(BF)
    s.grd[...] = slope
    slope32 = slope.astype(F32).reshape(2, 12, 16, 256)
    s.gt[1, pl.ds(0, 2), pl.ds(1, 12)] = slope.reshape(2, 12, 16, 256)
    for side, w in ((0, 0), (1, 15)):
        s.pgt[side] = pack(pick([slope32[t, :, w:w + 1] for t in range(2)]))
    halo_gt.start()

    def top_taps(abs_):
        lhs = jnp.concatenate(
            [s.xt[c, pl.ds(ab // 3, 2), pl.ds(ab % 3, 12)].reshape(384, 256)
             for ab in abs_ for c in range(3)], axis=1)
        return dot(lhs, s.grd[...], 0, 0).reshape(-1, 32, 8, 256)

    def top_store(r, first, second):
        both = jnp.concatenate([first, second], axis=1)
        s.terms[:, :, :, :, r] = both.astype(BF).reshape(4, 2, 2, 2, 16, 256)

    def top_six(i, _):
        group = top_taps([2 * i, 2 * i + 1])
        for k in range(3):
            top_store(3 * i + k, group[2 * k], group[2 * k + 1])
        return _

    if "tgrad" not in skip:
        lax.fori_loop(0, 4, top_six, 0)
    rs_top.start("a", 0, 10)
    group = top_taps([8])
    top_store(12, group[0], group[1])
    top_store(13, group[2], jnp.zeros((32, 8, 256), F32))
    rs_top.start("b", 10, TOP - 10)

    for kind in range(3):
        halo_gt.wait(kind)
    sides(halo_gt, s.gt)
    if "top" not in skip:
        top_conv(s.gt, True)
    rs_top.send("a")
    grad_red = (s.cot[...].astype(F32) + s.acc_t[...]).astype(BF)
    s.grd[...] = grad_red

    def store_low(r, lanes, group):
        first, second = weave(group[0], group[1]), weave(group[2], group[3])
        for par in range(2):
            both = jnp.concatenate([first[par], second[par]], axis=1).astype(BF)
            s.terms[:, :, :, par, r, :, lanes] = both.reshape(4, 2, 2, 16, both.shape[2])

    terms = dot(s.hf[...].reshape(1024, 384), s.grd[...]).reshape(8, 128, 256)
    for g in range(2):
        store_low(TOP + g, slice(0, 256), [terms[4 * g + i] for i in range(4)])
    rs_top.start("b", TOP, 2)

    spread = dot(grad_red, s.kd[...], 1, 1)
    for i, (a, b, c) in enumerate(taps):
        part = spread[:, i * 128:(i + 1) * 128].reshape(2, 12, 16, 128)
        for t in range(2):
            s.hg[2 * t + a, :, b, pl.ds(c, 16, stride=2), :] = part[t]

    low, high = [], []
    for t in range(4):
        gh = s.hg[t].reshape(24, 32, 128)
        slope = (gh * s.pre[t].reshape(24, 32, 128)).astype(BF)
        s.ge[t, pl.ds(1, 24)] = slope
        slope32 = slope.astype(F32)
        low.append(slope32[:, 0:1])
        high.append(slope32[:, 31:32])
        s.s3[t, :, 128:256] = slope.reshape(768, 128)
        s.s3[t, :, :128] = shift_cols(slope32, -1).astype(BF).reshape(768, 128)
        s.s3[t, :, 256:] = shift_cols(slope32, 1).astype(BF).reshape(768, 128)
    for side, parts in enumerate((low, high)):
        edge = pick(parts)
        s.pg[side] = pack(edge)
        s.sg[side] = edge.reshape(192, 128).astype(BF)
    halo_g.start()
    rs_top.send("b")

    def base_taps(a):
        lhs = s.xf[:, :, a * 768:a * 768 + 3072].reshape(384, 3072)
        total = dot(lhs, s.s3[...].reshape(3072, 384))
        s.acc[3 * a:3 * a + 3] = total.reshape(3, 128, 384)

    def base_sides(first, last):
        for side in range(2):
            extra = dot(s.colx[side, :, first * 128:last * 128], s.sg[side], 0, 0)
            lanes = slice(256 * side, 256 * side + 128)
            s.acc[first:last, :, lanes] = (
                s.acc[first:last, :, lanes] + extra.reshape(last - first, 128, 128))

    def base_groups(first, last):
        for g in range(first, last):
            group = []
            for tap in range(4 * g, 4 * g + 4):
                if tap < 27:
                    c = tap % 3
                    group.append(s.acc[tap // 3, :, c * 128:(c + 1) * 128])
                else:
                    group.append(jnp.zeros((128, 128), F32))
            lanes = slice(128 * (g % 2), 128 * (g % 2) + 128)
            store_low(TOP + 2 + g // 2, lanes, group)

    if "bgrad" not in skip:
        base_taps(0)
    rs_top.relay("a")
    if "bgrad" not in skip:
        base_taps(1)
    base_sides(0, 6)
    base_groups(0, 4)
    rs_low.start("a", TOP + 2, 2)
    if "bgrad" not in skip:
        base_taps(2)
    rs_top.relay("b")
    base_sides(6, 9)
    base_groups(4, 7)
    s.terms[:, :, :, :, ROWS - 1, :, 128:] = jnp.zeros((4, 2, 2, 2, 16, 128), BF)
    rs_low.start("b", TOP + 4, 2)
    rs_low.planes("a")
    rs_top.lines("a")

    for kind in range(3):
        halo_g.wait(kind)
    for side in range(2):
        column = halo_g.column(side)
        pieces = []
        for a in range(3):
            moved = pltpu.roll(column, 8 - a, 1) if a else column
            for b in range(3):
                pieces.append(moved[b:b + 24].reshape(192, 128).astype(BF))
        lhs = jnp.concatenate(pieces, axis=1)
        c = 2 * side
        s.hl[side] = dot(lhs, s.wb[c * 128:(c + 1) * 128, :], 1, 1)

    def backward(t):
        value = base_conv(s.ge, [(t, 0, 24)], s.wb[...], True)
        s.gfs[t] = s.hg[t].reshape(768, 128) + value
        for side in range(2):
            at = pl.ds(31 * side, 24, stride=32)
            s.gfs[t, at] = s.gfs[t, at] + s.hl[side, pl.ds(t, 24, stride=8)]
        copy = pltpu.make_async_copy(s.gfs.at[t], gf.at[t], s.leave.at[t])
        copy.start()
        leaving.append(copy)

    backward(0)
    rs_low.planes("b")
    rs_top.lines("b")
    backward(1)
    backward(2)
    rs_low.lines("a")
    rs_low.lines("b")
    rs_top.depth()
    backward(3)
    rs_low.depth()
    rs_top.finish_top(out_top, out_down, scales[1])
    rs_low.finish_base(out_base, scales[0])
    for copy in leaving:
        copy.wait()
    for user in (halo_x, halo_xt, halo_gt, halo_g, rs_top, rs_low):
        user.done()


def call(comm, skip, scales, *args):
    scratch = [pltpu.VMEM(*v) if isinstance(v, tuple) else v for v in scratch_list().values()]
    vmem = pl.BlockSpec(memory_space=pltpu.VMEM)
    params = dict(collective_id=0, has_side_effects=True) if comm else {}
    return pl.pallas_call(
        functools.partial(kernel, comm, skip, scales),
        out_shape=(
            jax.ShapeDtypeStruct((384, 256), BF),
            jax.ShapeDtypeStruct((4, 768, 128), F32),
            jax.ShapeDtypeStruct((16, 4, 27), F32),
            jax.ShapeDtypeStruct((8, 4, 32), F32),
            jax.ShapeDtypeStruct((27, 8, 32), F32),
        ),
        in_specs=[pl.BlockSpec(memory_space=pl.ANY)] * 5,
        out_specs=(pl.BlockSpec(memory_space=pl.ANY),) * 2 + (vmem,) * 3,
        scratch_shapes=scratch,
        compiler_params=pltpu.CompilerParams(vmem_limit_bytes=60 * 1024 * 1024, **params),
        cost_estimate=pl.CostEstimate(flops=13 * 10**9, bytes_accessed=10**7, transcendentals=10**6),
    )(*args)


def hand_over_kernel(*refs):
    n = (len(refs) - 2) // 3
    come, go = refs[-2:]
    pieces = []
    for src, dst, mid in zip(refs[:n], refs[n:2 * n], refs[2 * n:3 * n]):
        if src.shape[0] == 4:
            pieces += [(src.at[t], mid.at[t], dst.at[t]) for t in range(4)]
        else:
            pieces.append((src, mid, dst))
    inward = [pltpu.make_async_copy(a, b, come.at[i]) for i, (a, b, c) in enumerate(pieces)]
    outward = [pltpu.make_async_copy(b, c, go.at[i]) for i, (a, b, c) in enumerate(pieces)]
    for copy in inward:
        copy.start()
    for copy, after in zip(inward, outward):
        copy.wait()
        after.start()
    for copy in outward:
        copy.wait()


def hand_over(*arrays):
    n = len(arrays) + 3
    return pl.pallas_call(
        hand_over_kernel,
        out_shape=tuple(jax.ShapeDtypeStruct(a.shape, a.dtype) for a in arrays),
        in_specs=[pl.BlockSpec(memory_space=pl.ANY)] * len(arrays),
        out_specs=tuple(pl.BlockSpec(memory_space=pl.ANY) for _ in arrays),
        scratch_shapes=[pltpu.VMEM(a.shape, a.dtype) for a in arrays]
        + [pltpu.SemaphoreType.DMA((n,)), pltpu.SemaphoreType.DMA((n,))],
    )(*arrays)


def body(frames_in, kernel_base, kernel_down, kernel_top, cotangent, comm=True, skip=()):
    devices = 1
    if comm:
        devices = lax.axis_size("tm") * lax.axis_size("row") * lax.axis_size("col")
    scales = (1.0 / math.sqrt(devices * 3072), 1.0 / math.sqrt(devices * 384))
    feat, gf, base, down, top = call(
        comm, skip, scales,
        frames_in,
        kernel_base.reshape(9, 3, 128, 128),
        kernel_down.reshape(1024, 256),
        kernel_top.reshape(27, 256, 256),
        cotangent.reshape(384, 256),
    )
    gf, feat, base, down, top = hand_over(gf, feat, base, down, top)
    return (
        feat.reshape(2, 12, 16, 256),
        gf.reshape(4, 24, 32, 128),
        base.transpose(2, 0, 1),
        down.transpose(0, 2, 1),
        top.transpose(0, 2, 1),
    )


def solution(mesh):
    return jax.shard_map(
        body,
        mesh=mesh,
        in_specs=(P("tm", "row", "col", None), P(), P(), P(), P("tm", "row", "col", None)),
        out_specs=(
            P("tm", "row", "col", None),
            P("tm", "row", "col", None),
            P(None, "col", ("tm", "row")),
            P(None, "col", ("tm", "row")),
            P(None, "col", ("tm", "row")),
        ),
        check_vma=False,
    )
```
